32 devices in a mesh: row: 16 (over z, x, core), off: 2 (over y).
Axes of the slice: x: 2, y: 2, z: 4, core: 2. Of those that a mesh axis runs over, the one named last changes fastest.
Arguments:
- vectors: float32 [64, 16384], P(None, 'row'), may hold values from -6 to 6
- tiles: float32 [16384, 4096], P('row', 'off'), may hold values from -0.0625 to 0.0625
- live: int32 [16, 4], P('row', 'off'), may hold values from 256 to 1024
- energies: float32 [16384], P('row'), may hold values from 0.25 to 5.25
- precond: float32 [16384], P('row'), may hold values from 0.03 to 0.3
Outputs:
- basis: float32 [64, 16384], P(None, 'row')
- ritz: float32 [64, 64], replicated
The draws below stay inside these ranges and needn't reach their ends.
All inputs are finite; a program needn't handle non-finite values.
Results may differ from the reference program's by a relative error of at most 0.00025.
Values sent between devices are 32-bit elements; how exact they have to be, the bound alone decides.
A program may use at most 64 MiB of HBM per device.

```python
import math
import jax
import jax.numpy as jnp
from jax import lax

K = 64
G = 1024
ITERS = 2
NOFF = 4
NROWS = 16384


def draw_energies(key, part):
    group_ids = (jnp.arange(NROWS) // G).astype(jnp.float32)
    ladder = 1.0 + 2.0 * group_ids / (NROWS // G - 1)
    factor = jax.random.uniform(key, (NROWS,), jnp.float32, 0.5, 1.5)
    return ladder * factor


def draw_live(key, part):
    entries = NROWS // G * NOFF
    key_vals, key_spot = jax.random.split(jax.random.fold_in(key, 17))
    flat = jax.random.randint(key_vals, (entries,), G // 4, G + 1)
    spot_index = jax.random.randint(key_spot, (), 0, entries)
    flat = flat.at[spot_index].set(G)
    flat = flat.at[(spot_index + 1) % entries].set(G // 4)
    return flat.reshape(entries // NOFF, NOFF).astype(jnp.int32)


def block_levels(stream_key, dims, cuts, smallest, high):
    def one(position, blocks):
        heights = jax.random.uniform(jax.random.fold_in(jax.random.fold_in(stream_key, 6), position), (blocks,), jnp.float32, smallest / len(cuts), high / len(cuts))
        return jnp.repeat(jnp.exp(heights), dims[position] // blocks).reshape((-1,) + (1,) * (len(dims) - position - 1))

    factor_of = one(*cuts[0])
    for cut in cuts[1:]:
        factor_of = factor_of * one(*cut)
    return factor_of


def bell_draw(key, shape, deviation, bound, shards=(), held_as=jnp.bfloat16):
    result = deviation * jax.random.normal(key, shape, jnp.float32)
    if shards:
        result = result * block_levels(key, shape, shards, -0.22, 0.18)
    return jnp.clip(result, -bound, bound).astype(held_as)


def setup_inputs(seed: int = 0) -> dict:
    arg_keys = jax.random.split(jax.random.key(seed), 6)
    vectors = bell_draw(arg_keys[0], (K, NROWS), 1.0, 6.0, ((1, 16),), jnp.float32)
    tiles = bell_draw(arg_keys[1], (NROWS, NOFF * G), (2 * NOFF * G) ** -0.5, 0.0625, ((0, 16), (1, 2)), jnp.float32)
    live = draw_live(jax.random.fold_in(arg_keys[5], 71), 0)
    energies = draw_energies(jax.random.fold_in(arg_keys[5], 71), 0)
    precond = jnp.clip(jnp.exp(math.log(0.3) - 2.3025852 * jax.random.uniform(arg_keys[4], (NROWS,), jnp.float32) ** block_levels(arg_keys[4], (NROWS,), ((0, 16),), -0.2, 0.2)), 0.03, 0.3)
    return dict(vectors=vectors, tiles=tiles, live=live, energies=energies, precond=precond)


def apply_ham(vectors, tiles, live, energies):
    ngroups = NROWS // G
    split = vectors.reshape(K, ngroups, G)
    blocks = tiles.reshape(ngroups, G, NOFF, G)
    row_ids = jnp.arange(G, dtype=jnp.int32)
    direct = jnp.zeros_like(split)
    returned = jnp.zeros_like(split)
    for offset in range(NOFF):
        keep = (row_ids[None, :] < live[:, offset][:, None]).astype(jnp.float32)
        block = blocks[:, :, offset, :] * keep[:, :, None]
        shifted = jnp.roll(split, -offset, axis=1)
        direct = direct + jnp.einsum("igc,kic->kig", block, shifted, precision=lax.Precision.HIGHEST)
        back = jnp.einsum("igc,kig->kic", block, split, precision=lax.Precision.HIGHEST)
        returned = returned + jnp.roll(back, offset, axis=1)
    return energies * vectors + (direct + returned).reshape(K, NROWS)


def product(left, right):
    return jnp.dot(left, right, precision=lax.Precision.HIGHEST, preferred_element_type=jnp.float32)


def reference(vectors, tiles, live, energies, precond):
    identity = jnp.eye(K, dtype=jnp.float32)
    ritz_matrix = jnp.zeros((K, K), jnp.float32)
    for iteration in range(ITERS):
        image = apply_ham(vectors, tiles, live, energies)
        ritz_matrix = product(vectors, image.T) / NROWS
        resid = image - product(ritz_matrix.T, vectors)
        moved = vectors - precond * resid
        correlation = product(moved, moved.T) / NROWS
        vectors = product((1.5 * identity - 0.5 * correlation).T, moved)
    return vectors, ritz_matrix
```

```python
import functools

import jax
import jax.numpy as jnp
from jax import lax
from jax.experimental import pallas as pl
from jax.experimental.pallas import tpu as pltpu
from jax.sharding import PartitionSpec as P

ITERS = 2
MESH = pl.DeviceIdType.MESH
HIGHEST = lax.Precision.HIGHEST
NN = (((1,), (0,)), ((), ()))
NT = (((1,), (1,)), ((), ()))


def exact(left, right, dims=NN):
    return lax.dot_general(
        left, right, dims, precision=HIGHEST, preferred_element_type=jnp.float32
    )


def coarse(left, right, dims):
    return lax.dot_general(left, right, dims, preferred_element_type=jnp.float32)


def halves(value):
    high = value.astype(jnp.bfloat16)
    low = (value - high.astype(jnp.float32)).astype(jnp.bfloat16)
    return high, low


def kernel(
    n, n_off, slots, total_rows,
    vec_ref, tiles_ref, live_ref, energy_ref, precond_ref,
    out_ref, ritz_ref,
    raw, high, low, mine, near, split, direct, back, ret, part_a, own_a, near_a,
    gram, gram_in, gram_off, gram_sum, gram_all,
    load_sem, fetch_send, fetch_recv, ret_send, ret_recv, share_send, share_recv,
    peer_send, peer_recv, gs_send, gs_recv, go_send, go_recv, ga_send, ga_recv,
):
    me = lax.axis_index("row")
    off = lax.axis_index("off")
    k, width = vec_ref.shape
    part = width // n_off
    chunk = min(256, part)
    grow = 2 * k // n

    def copy(src, dst, send, recv, row, col):
        return pltpu.make_async_remote_copy(
            src_ref=src, dst_ref=dst, send_sem=send, recv_sem=recv,
            device_id=(row, col), device_id_type=MESH,
        )

    def row_at(shift):
        return lax.rem(me + shift + n, n)

    def peer(step):
        return lax.rem(off + step, n_off)

    def cols(index):
        return pl.ds(pl.multiple_of(index * part, part), part)

    loads = []
    for slot in range(slots):
        load = pltpu.make_async_copy(
            tiles_ref.at[:, pl.ds(slot * width, width)], raw.at[slot], load_sem.at[slot]
        )
        load.start()
        loads.append(load)

    barrier = pltpu.get_barrier_semaphore()

    def greet(step, carry):
        flat = lax.rem(me * n_off + off + step, n * n_off)
        pl.semaphore_signal(
            barrier, inc=1, device_id=(flat // n_off, lax.rem(flat, n_off)),
            device_id_type=MESH,
        )
        return carry

    lax.fori_loop(1, n * n_off, greet, 0)
    mine[:k, :] = vec_ref[...]
    mine[k:, :] = jnp.broadcast_to(precond_ref[...], (mine.shape[0] - k, width))
    pl.semaphore_wait(barrier, n * n_off - 1)

    def spread(src, dst, send, recv):
        started = []
        for group in range(n_off):
            for slot in range(slots):
                shift = group * slots + slot
                if shift:
                    one = copy(
                        src, dst.at[slot, :, cols(off)], send.at[shift],
                        recv.at[slot, off], row_at(-shift), group,
                    )
                    one.start()
                    started.append(one)
        return started

    def gathered(slot, dst, recv):
        for step in range(n_off):
            where = dst.at[slot, :, cols(step)]
            copy(where, where, recv.at[slot, step], recv.at[slot, step],
                 row_at(1), off).wait_recv()

    sent = spread(mine.at[:, cols(off)], near, fetch_send, fetch_recv)

    def put_split(where, value):
        hi, lo = halves(value)
        split[where, :k, :] = hi
        split[where, k:, :] = lo

    put_split(slots, vec_ref[...])

    def transposed(it, slot):
        shift = off * slots + slot
        for q in range(n_off):
            for c in range(part // chunk):
                at = pl.ds(q * part + c * chunk, chunk)
                both = coarse(split[slots], high[slot, :, at], NN)
                rest = coarse(split[slots, :k, :], low[slot, :, at], NN)
                back[it, slot, q, :, pl.ds(c * chunk, chunk)] = both[:k] + both[k:] + rest

            @pl.when(shift != 0)
            def _():
                copy(
                    back.at[it, slot, q], ret.at[it, off, slot],
                    ret_send.at[it, slot, q], ret_recv.at[it, off, slot],
                    row_at(shift), q,
                ).start()

    def forward(it, slot, first):
        for c in range(width // chunk):
            at = pl.ds(c * chunk, chunk)
            both = coarse(split[slot], high[slot, at, :], NT)
            rest = coarse(split[slot, :k, :], low[slot, at, :], NT)
            term = both[:k] + both[k:] + rest
            q, place = (c * chunk) // part, (c * chunk) % part
            where = pl.ds(place, chunk)
            if first:
                direct[it, q, :, where] = term
            else:
                direct[it, q, :, where] = direct[it, q, :, where] + term

    order = list(range(slots - 1, -1, -1))
    rows = 32
    for slot in order:
        loads[slot].wait()
        limit = live_ref[0, slot]

        def cut(index, carry):
            start = pl.multiple_of(index * rows, rows)
            ids = lax.broadcasted_iota(jnp.int32, (rows, width), 0) + start
            value = jnp.where(ids < limit, raw[slot, pl.ds(start, rows), :], 0.0)
            hi, lo = halves(value)
            high[slot, pl.ds(start, rows), :] = hi
            low[slot, pl.ds(start, rows), :] = lo
            return carry

        lax.fori_loop(0, width // rows, cut, 0)
        transposed(0, slot)

    for slot in order:
        if slot == 0:
            @pl.when(off == 0)
            def _():
                split[0] = split[slots]
                near[0] = mine[...]

            @pl.when(off != 0)
            def _():
                gathered(0, near, fetch_recv)
                put_split(0, near[0, :k, :])
        else:
            gathered(slot, near, fetch_recv)
            put_split(slot, near[slot, :k, :])

    def eye():
        return (
            lax.broadcasted_iota(jnp.int32, (k, k), 0)
            == lax.broadcasted_iota(jnp.int32, (k, k), 1)
        ).astype(jnp.float32)

    state = mine
    for it in range(ITERS):
        last = it == ITERS - 1
        for position, slot in enumerate(order):
            forward(it, slot, position == 0)

        @pl.when(off == 0)
        def _():
            for q in range(n_off):
                direct[it, q] = direct[it, q] + back[it, 0, q]

        for step in range(1, n_off):
            copy(
                direct.at[it, peer(step)], ret.at[it, off, slots],
                ret_send.at[it, slots, step], ret_recv.at[it, off, slots],
                me, peer(step),
            ).start()

        x_part = state[:k, cols(off)]
        p_part = precond_ref[:, cols(off)]
        total = energy_ref[:, cols(off)] * x_part + direct[it, off]
        for group in range(n_off):
            for slot in range(slots):
                if group or slot:
                    where = ret.at[it, group, slot]
                    copy(where, where, ret_send.at[it, 0, 0], ret_recv.at[it, group, slot],
                         row_at(1), off).wait_recv()
                    total = total + ret[it, group, slot]
        for step in range(1, n_off):
            where = ret.at[it, peer(step), slots]
            copy(where, where, ret_send.at[it, 0, 0], ret_recv.at[it, peer(step), slots],
                 row_at(1), off).wait_recv()
            total = total + ret[it, peer(step), slots]

        a_part = x_part - p_part * total
        part_a[it] = a_part
        own_a[it, :, cols(off)] = a_part
        for step in range(1, n_off):
            copy(
                part_a.at[it], own_a.at[it, :, cols(off)],
                peer_send.at[it, step], peer_recv.at[it, off], me, peer(step),
            ).start()
        if not last:
            sent += spread(part_a.at[it], near_a, share_send, share_recv)

        ab = jnp.concatenate([a_part, p_part * x_part], axis=0)
        inner = exact(ab, ab, NT)
        xy = exact(x_part, total, NT)
        low_half = jnp.concatenate([xy, inner[k:, k:]], axis=1)
        packed = jnp.concatenate([inner[:k, :], low_half], axis=0)
        for t in range(n):
            gram[it, t] = packed[t * grow : (t + 1) * grow, :]

        for step in range(1, n):
            target = row_at(step)
            copy(
                gram.at[it, target], gram_in.at[it, me], gs_send.at[it, step],
                gs_recv.at[it, me], target, off,
            ).start()
        piece = gram[it, me]
        for step in range(1, n):
            source = row_at(step)
            where = gram_in.at[it, source]
            copy(where, where, gs_send.at[it, step], gs_recv.at[it, source],
                 row_at(1), off).wait_recv()
            piece = piece + gram_in[it, source]
        gram_off[it, off] = piece
        for step in range(1, n_off):
            copy(
                gram_off.at[it, off], gram_off.at[it, off], go_send.at[it, step],
                go_recv.at[it, off], me, peer(step),
            ).start()
        for step in range(1, n_off):
            where = gram_off.at[it, peer(step)]
            copy(where, where, go_send.at[it, step], go_recv.at[it, peer(step)],
                 row_at(1), off).wait_recv()
        piece = gram_off[it, 0]
        for q in range(1, n_off):
            piece = piece + gram_off[it, q]
        gram_sum[it] = piece
        gram_all[it, me] = piece
        for step in range(1, n):
            copy(
                gram_sum.at[it], gram_all.at[it, me], ga_send.at[it, step],
                ga_recv.at[it, me], row_at(step), off,
            ).start()
        for step in range(1, n):
            source = row_at(step)
            where = gram_all.at[it, source]
            copy(where, where, ga_send.at[it, step], ga_recv.at[it, source],
                 row_at(1), off).wait_recv()
        full = jnp.concatenate([gram_all[it, t] for t in range(n)], axis=0) / total_rows
        turned = full.T
        ritz, ritz_t = full[k:, :k], turned[:k, k:]
        aa, cross, cross_t, bb = full[:k, :k], full[:k, k:], turned[k:, :k], full[k:, k:]
        mixed = exact(cross, ritz)
        overlap = aa + mixed + exact(ritz_t, cross_t + exact(bb, ritz))
        fix = 1.5 * eye() - 0.5 * overlap
        both_fix = jnp.concatenate([fix, exact(fix, ritz_t)], axis=1)

        def update(a_value, x_value, p_row):
            return exact(both_fix, jnp.concatenate([a_value, p_row * x_value], axis=0))

        for step in range(1, n_off):
            where = own_a.at[it, :, cols(peer(step))]
            copy(where, where, peer_send.at[it, step], peer_recv.at[it, peer(step)],
                 row_at(1), off).wait_recv()
        fresh = update(own_a[it], state[:k, :], precond_ref[...])
        out_ref[...] = fresh
        if last:
            ritz_ref[...] = ritz
        else:
            put_split(slots, fresh)
            for slot in order:
                transposed(it + 1, slot)

            def renew(slot):
                gathered(slot, near_a, share_recv)
                value = update(
                    near_a[slot], near[slot, :k, :], near[slot, k : k + 1, :]
                )
                near[slot, :k, :] = value
                put_split(slot, value)

            for slot in order:
                if slot == 0:
                    @pl.when(off == 0)
                    def _():
                        split[0] = split[slots]

                    @pl.when(off != 0)
                    def _():
                        renew(0)
                else:
                    renew(slot)
            state = out_ref

    for one in sent:
        one.wait_send()
    for it in range(ITERS):
        for slot in range(slots):
            for q in range(n_off):
                @pl.when(off * slots + slot != 0)
                def _():
                    copy(back.at[it, slot, q], ret.at[it, off, slot], ret_send.at[it, slot, q],
                         ret_recv.at[it, off, slot], row_at(1), q).wait_send()
        for step in range(1, n_off):
            copy(direct.at[it, 0], ret.at[it, off, slots], ret_send.at[it, slots, step],
                 ret_recv.at[it, off, slots], me, peer(step)).wait_send()
            copy(part_a.at[it], part_a.at[it], peer_send.at[it, step],
                 peer_recv.at[it, off], me, peer(step)).wait_send()
            copy(gram_sum.at[it], gram_sum.at[it], go_send.at[it, step],
                 go_recv.at[it, off], me, peer(step)).wait_send()
        for step in range(1, n):
            copy(gram_sum.at[it], gram_sum.at[it], gs_send.at[it, step],
                 gs_recv.at[it, me], row_at(step), off).wait_send()
            copy(gram_sum.at[it], gram_sum.at[it], ga_send.at[it, step],
                 ga_recv.at[it, me], row_at(step), off).wait_send()


def local(n, n_off, vectors, tiles, live, energies, precond):
    k, width = vectors.shape
    slots = tiles.shape[1] // width
    part = width // n_off
    grow = 2 * k // n
    f32, b16 = jnp.float32, jnp.bfloat16
    vmem, dma = pltpu.VMEM, pltpu.SemaphoreType.DMA
    inside = pl.BlockSpec(memory_space=pltpu.VMEM)
    return pl.pallas_call(
        functools.partial(kernel, n, n_off, slots, float(width * n)),
        out_shape=(
            jax.ShapeDtypeStruct((k, width), f32),
            jax.ShapeDtypeStruct((k, k), f32),
        ),
        in_specs=[
            inside,
            pl.BlockSpec(memory_space=pl.ANY),
            pl.BlockSpec(memory_space=pltpu.SMEM),
            inside,
            inside,
        ],
        out_specs=(inside, inside),
        scratch_shapes=[
            vmem((slots, width, width), f32),
            vmem((slots, width, width), b16),
            vmem((slots, width, width), b16),
            vmem((k + 8, width), f32),
            vmem((slots, k + 8, width), f32),
            vmem((slots + 1, 2 * k, width), b16),
            vmem((ITERS, n_off, k, part), f32),
            vmem((ITERS, slots, n_off, k, part), f32),
            vmem((ITERS, n_off, slots + 1, k, part), f32),
            vmem((ITERS, k, part), f32),
            vmem((ITERS, k, width), f32),
            vmem((slots, k, width), f32),
            vmem((ITERS, n, grow, 2 * k), f32),
            vmem((ITERS, n, grow, 2 * k), f32),
            vmem((ITERS, n_off, grow, 2 * k), f32),
            vmem((ITERS, grow, 2 * k), f32),
            vmem((ITERS, n, grow, 2 * k), f32),
            dma((slots,)),
            dma((n_off * slots,)),
            dma((slots, n_off)),
            dma((ITERS, slots + 1, n_off)),
            dma((ITERS, n_off, slots + 1)),
            dma((n_off * slots,)),
            dma((slots, n_off)),
            dma((ITERS, n_off)),
            dma((ITERS, n_off)),
            dma((ITERS, n)),
            dma((ITERS, n)),
            dma((ITERS, n_off)),
            dma((ITERS, n_off)),
            dma((ITERS, n)),
            dma((ITERS, n)),
        ],
        compiler_params=pltpu.CompilerParams(
            collective_id=0, has_side_effects=True, vmem_limit_bytes=48 * 1024 * 1024
        ),
    )(vectors, tiles, live, energies[None, :], precond[None, :])


def solution(mesh):
    placed = (P(None, "row"), P("row", "off"), P("row", "off"), P("row"), P("row"))
    return jax.shard_map(
        functools.partial(local, mesh.shape["row"], mesh.shape["off"]),
        mesh=mesh, in_specs=placed, out_specs=(P(None, "row"), P()), check_vma=False,
    )
```

```python
import functools

import jax
import jax.numpy as jnp
from jax import lax
from jax.experimental import pallas as pl
from jax.experimental.pallas import tpu as pltpu
from jax.sharding import PartitionSpec as P

ITERS = 2
MESH = pl.DeviceIdType.MESH
NN = (((1,), (0,)), ((), ()))
NT = (((1,), (1,)), ((), ()))


def coarse(left, right, dims):
    return lax.dot_general(left, right, dims, preferred_element_type=jnp.float32)


def halves(value):
    high = value.astype(jnp.bfloat16)
    low = (value - high.astype(jnp.float32)).astype(jnp.bfloat16)
    return high, low


def triple(left, right, dims=NN):
    left_hi, left_lo = halves(left)
    right_hi, right_lo = halves(right)
    count = left.shape[0]
    both = coarse(jnp.concatenate([left_hi, left_lo], axis=0), right_hi, dims)
    return both[:count] + both[count:] + coarse(left_hi, right_lo, dims)


def kernel(
    n, n_off, slots, total_rows,
    vec_hbm, tiles_ref, live_hbm, energy_hbm, precond_hbm,
    out_ref, ritz_ref,
    vec_ref, live_ref, energy_ref, precond_ref, acc, hand,
    raw, high, low, mine, near, split, direct, back, ret, part_a, own_a, near_a,
    gram, gram_in, gram_sum, gram_all,
    load_sem, hand_recv, fetch_relay, share_relay, fetch_send, fetch_recv, ret_send, ret_recv, share_send, share_recv,
    peer_send, peer_recv, gs_send, gs_recv, ga_send, ga_recv,
):
    me = lax.axis_index("row")
    off = lax.axis_index("off")
    k, width = vec_ref.shape
    part = width // n_off
    chunk = min(256, part)
    owners = min(n_off, 2 * k // n)
    grow = 2 * k // (n * owners)
    devices = n * n_off
    flat_me = me * n_off + off
    odd = lax.rem(me, 2) == 1
    small = devices <= 32

    def copy(src, dst, send, recv, row, col):
        return pltpu.make_async_remote_copy(
            src_ref=src, dst_ref=dst, send_sem=send, recv_sem=recv,
            device_id=(row, col), device_id_type=MESH,
        )

    def row_at(shift):
        return lax.rem(me + shift + n, n)

    def peer(step):
        return lax.rem(off + step, n_off)

    def cols(index):
        return pl.ds(pl.multiple_of(index * part, part), part)

    heads = [
        pltpu.make_async_copy(src, dst, load_sem.at[slots + index])
        for index, (src, dst) in enumerate(
            ((vec_hbm, vec_ref), (precond_hbm, precond_ref),
             (energy_hbm, energy_ref), (live_hbm, live_ref))
        )
    ]
    for one in heads:
        one.start()
    order = list(range(slots - 1, -1, -1))
    loads = [
        pltpu.make_async_copy(
            tiles_ref.at[:, pl.ds(slot * width, width)], raw.at[slot], load_sem.at[slot]
        )
        for slot in range(slots)
    ]
    for slot in order:
        loads[slot].start()

    barrier = pltpu.get_barrier_semaphore()

    def greet(step, carry):
        flat = lax.rem(flat_me + step, devices)
        pl.semaphore_signal(
            barrier, inc=1, device_id=(flat // n_off, lax.rem(flat, n_off)),
            device_id_type=MESH,
        )
        return carry

    lax.fori_loop(1, devices, greet, 0, unroll=small)
    for one in heads:
        one.wait()
    mine[:k, :] = vec_ref[...]
    mine[k:, :] = jnp.broadcast_to(precond_ref[...], (mine.shape[0] - k, width))
    pl.semaphore_wait(barrier, devices - 1)

    def spread(src, dst, send, recv, act):
        for group in range(n_off):
            for slot in range(slots):
                shift = group * slots + slot

                def step():
                    one = copy(
                        src, dst.at[slot, :, cols(off)], send.at[shift],
                        recv.at[slot, off], row_at(-shift), group,
                    )
                    act(one)

                if slot:
                    pl.when(lax.rem(me + shift, 2) == 1)(step)
                elif shift:
                    step()

    def relay(dst, send, recv, act):
        @pl.when(odd)
        def _():
            for slot in range(slots - 1):
                for q in range(n_off):
                    act(copy(
                        dst.at[slot, :, cols(q)], dst.at[slot + 1, :, cols(q)],
                        send.at[slot, q], recv.at[slot + 1, q], row_at(-1), off,
                    ))

    def begin(one):
        one.start()

    def finish(one):
        one.wait_send()

    def gathered(slot, dst, recv):
        for step in range(n_off):
            where = dst.at[slot, :, cols(step)]
            copy(where, where, recv.at[slot, step], recv.at[slot, step],
                 row_at(1), off).wait_recv()

    spread(mine.at[:, cols(off)], near, fetch_send, fetch_recv, begin)

    def put_split(where, value):
        hi, lo = halves(value)
        split[where, :k, :] = hi
        split[where, k:, :] = lo

    put_split(slots, vec_ref[...])

    def transposed(it, slot):
        shift = off * slots + slot
        for q in range(n_off):
            for c in range(part // chunk):
                at = pl.ds(q * part + c * chunk, chunk)
                both = coarse(split[slots], high[slot, :, at], NN)
                rest = coarse(split[slots, :k, :], low[slot, :, at], NN)
                back[it, slot, q, :, pl.ds(c * chunk, chunk)] = both[:k] + both[k:] + rest

            if slot < slots - 1:
                @pl.when(odd)
                def _():
                    where = hand.at[it, slot, q]
                    copy(where, where, hand_recv.at[it, slot, q], hand_recv.at[it, slot, q],
                         row_at(1), off).wait_recv()
                    back[it, slot, q] = back[it, slot, q] + hand[it, slot, q]

            def away():
                copy(
                    back.at[it, slot, q], ret.at[it, off, slot],
                    ret_send.at[it, slot, q], ret_recv.at[it, off, slot],
                    row_at(shift), q,
                ).start()

            if slot:
                pl.when(odd)(away)

                @pl.when(jnp.logical_not(odd))
                def _():
                    copy(
                        back.at[it, slot, q], hand.at[it, slot - 1, q],
                        ret_send.at[it, slot, q], hand_recv.at[it, slot - 1, q],
                        row_at(1), off,
                    ).start()
            else:
                pl.when(shift != 0)(away)

    def forward(it, slot, first):
        for c in range(width // chunk):
            at = pl.ds(c * chunk, chunk)
            both = coarse(split[slot], high[slot, at, :], NT)
            rest = coarse(split[slot, :k, :], low[slot, at, :], NT)
            term = both[:k] + both[k:] + rest
            q, place = (c * chunk) // part, (c * chunk) % part
            where = pl.ds(place, chunk)
            if first:
                direct[it, q, :, where] = term
            else:
                direct[it, q, :, where] = direct[it, q, :, where] + term

    rows = 32
    for slot in order:
        loads[slot].wait()
        limit = live_ref[0, slot]

        def cut(index, carry):
            start = pl.multiple_of(index * rows, rows)
            ids = lax.broadcasted_iota(jnp.int32, (rows, width), 0) + start
            value = jnp.where(ids < limit, raw[slot, pl.ds(start, rows), :], 0.0)
            hi, lo = halves(value)
            high[slot, pl.ds(start, rows), :] = hi
            low[slot, pl.ds(start, rows), :] = lo
            return carry

        lax.fori_loop(0, width // rows, cut, 0)
        transposed(0, slot)

    def collect(dst, own, send, recv, use):
        for slot in range(slots):
            if slot == 0:
                @pl.when(off == 0)
                def _():
                    dst[0] = own[...]

                @pl.when(off != 0)
                def _():
                    gathered(0, dst, recv)
            else:
                gathered(slot, dst, recv)
            if slot == slots - 2:
                relay(dst, send, recv, begin)
            use(slot)

    def eye():
        return (
            lax.broadcasted_iota(jnp.int32, (k, k), 0)
            == lax.broadcasted_iota(jnp.int32, (k, k), 1)
        ).astype(jnp.float32)

    state = mine
    for it in range(ITERS):
        last = it == ITERS - 1
        if it == 0:
            def use(slot):
                put_split(slot, near[slot, :k, :])
                forward(0, slot, slot == 0)

            collect(near, mine, fetch_relay, fetch_recv, use)

        @pl.when(off == 0)
        def _():
            for q in range(n_off):
                direct[it, q] = direct[it, q] + back[it, 0, q]

        for step in range(1, n_off):
            copy(
                direct.at[it, peer(step)], ret.at[it, off, slots],
                ret_send.at[it, slots, step], ret_recv.at[it, off, slots],
                me, peer(step),
            ).start()

        x_part = state[:k, cols(off)]
        p_part = precond_ref[:, cols(off)]
        acc[...] = energy_ref[:, cols(off)] * x_part + direct[it, off]
        for group in range(n_off):
            for slot in range(slots):
                def take():
                    where = ret.at[it, group, slot]
                    copy(where, where, ret_send.at[it, 0, 0], ret_recv.at[it, group, slot],
                         row_at(1), off).wait_recv()
                    acc[...] = acc[...] + ret[it, group, slot]

                if slot:
                    pl.when(lax.rem(me + group * slots + slot, 2) == 1)(take)
                elif group:
                    take()
        total = acc[...]
        for step in range(1, n_off):
            where = ret.at[it, peer(step), slots]
            copy(where, where, ret_send.at[it, 0, 0], ret_recv.at[it, peer(step), slots],
                 row_at(1), off).wait_recv()
            total = total + ret[it, peer(step), slots]

        a_part = x_part - p_part * total
        part_a[it] = a_part
        own_a[it, :, cols(off)] = a_part
        for step in range(1, n_off):
            copy(
                part_a.at[it], own_a.at[it, :, cols(off)],
                peer_send.at[it, step], peer_recv.at[it, off], me, peer(step),
            ).start()
        if not last:
            spread(part_a.at[it], near_a, share_send, share_recv, begin)

        ab = jnp.concatenate([a_part, p_part * x_part], axis=0)
        inner = triple(ab, ab, NT)
        xy = triple(x_part, total, NT)
        low_half = jnp.concatenate([xy, inner[k:, k:]], axis=1)
        packed = jnp.concatenate([inner[:k, :], low_half], axis=0)
        for t in range(n * owners):
            gram[it, t] = packed[t * grow : (t + 1) * grow, :]

        def owner_at(step):
            index = lax.rem(me * owners + lax.rem(off, owners) + step, n * owners)
            return index, index // owners, lax.rem(index, owners)

        def deal(step, carry):
            index, row, col = owner_at(step)
            copy(
                gram.at[it, index], gram_in.at[it, flat_me], gs_send.at[it, index],
                gs_recv.at[it, flat_me], row, col,
            ).start()
            return carry

        def add(step, piece):
            source = lax.rem(flat_me + step, devices)
            where = gram_in.at[it, source]
            copy(where, where, gs_send.at[it, 0], gs_recv.at[it, source],
                 row_at(1), off).wait_recv()
            return piece + gram_in[it, source]

        def tell(step, carry):
            target = lax.rem(flat_me + step, devices)
            copy(
                gram_sum.at[it], gram_all.at[it, me * owners + off], ga_send.at[it, target],
                ga_recv.at[it, me * owners + off], target // n_off, lax.rem(target, n_off),
            ).start()
            return carry

        def hear(step, carry):
            index = owner_at(step)[0]
            where = gram_all.at[it, index]
            copy(where, where, ga_send.at[it, 0], ga_recv.at[it, index],
                 row_at(1), off).wait_recv()
            return carry

        def own():
            piece = lax.fori_loop(
                1, devices, add, gram[it, me * owners + off], unroll=small
            )
            gram_sum[it] = piece
            gram_all[it, me * owners + off] = piece
            lax.fori_loop(1, devices, tell, 0, unroll=small)

        lax.fori_loop(1, n * owners, deal, 0, unroll=small)
        if owners == n_off:
            own()
        else:
            pl.when(off < owners)(own)

            @pl.when(off >= owners)
            def _():
                deal(0, 0)
                hear(0, 0)

        lax.fori_loop(1, n * owners, hear, 0, unroll=small)
        full = gram_all[it].reshape(2 * k, 2 * k) / total_rows
        turned = full.T
        ritz, ritz_t = full[k:, :k], turned[:k, k:]
        aa, cross, cross_t, bb = full[:k, :k], full[:k, k:], turned[k:, :k], full[k:, k:]
        mixed = triple(jnp.concatenate([cross, bb], axis=0), ritz)
        overlap = aa + mixed[:k] + triple(ritz_t, cross_t + mixed[k:])
        fix = 1.5 * eye() - 0.5 * overlap
        both_fix = jnp.concatenate([fix, triple(fix, ritz_t)], axis=1)

        def update(a_value, x_value, p_row):
            return triple(both_fix, jnp.concatenate([a_value, p_row * x_value], axis=0))

        for step in range(1, n_off):
            where = own_a.at[it, :, cols(peer(step))]
            copy(where, where, peer_send.at[it, step], peer_recv.at[it, peer(step)],
                 row_at(1), off).wait_recv()
        fresh = update(own_a[it], state[:k, :], precond_ref[...])
        out_ref[...] = fresh
        if last:
            ritz_ref[...] = ritz
        else:
            put_split(slots, fresh)
            for slot in order:
                transposed(it + 1, slot)

            def renew(slot):
                value = update(
                    near_a[slot], near[slot, :k, :], near[slot, k : k + 1, :]
                )
                put_split(slot, value)
                forward(it + 1, slot, slot == 0)

            collect(near_a, own_a.at[it], share_relay, share_recv, renew)
            state = out_ref

    spread(mine.at[:, cols(off)], near, fetch_send, fetch_recv, finish)
    relay(near, fetch_relay, fetch_recv, finish)
    spread(part_a.at[0], near_a, share_send, share_recv, finish)
    relay(near_a, share_relay, share_recv, finish)
    for it in range(ITERS):
        for slot in range(slots):
            for q in range(n_off):
                def gone():
                    copy(back.at[it, slot, q], ret.at[it, off, slot], ret_send.at[it, slot, q],
                         ret_recv.at[it, off, slot], row_at(1), q).wait_send()

                if slot:
                    gone()
                else:
                    pl.when(off != 0)(gone)
        for step in range(1, n_off):
            copy(direct.at[it, 0], ret.at[it, off, slots], ret_send.at[it, slots, step],
                 ret_recv.at[it, off, slots], me, peer(step)).wait_send()
            copy(part_a.at[it], part_a.at[it], peer_send.at[it, step],
                 peer_recv.at[it, off], me, peer(step)).wait_send()

        def dealt(step, carry):
            index = lax.rem(me * owners + lax.rem(off, owners) + step, n * owners)
            copy(gram_sum.at[it], gram_sum.at[it], gs_send.at[it, index],
                 gs_recv.at[it, 0], row_at(1), off).wait_send()
            return carry

        def told(step, carry):
            target = lax.rem(flat_me + step, devices)
            copy(gram_sum.at[it], gram_sum.at[it], ga_send.at[it, target],
                 ga_recv.at[it, 0], row_at(1), off).wait_send()
            return carry

        lax.fori_loop(1, n * owners, dealt, 0, unroll=small)
        if owners == n_off:
            lax.fori_loop(1, devices, told, 0, unroll=small)
        else:
            @pl.when(off < owners)
            def _():
                lax.fori_loop(1, devices, told, 0)

            @pl.when(off >= owners)
            def _():
                dealt(0, 0)


def local(n, n_off, vectors, tiles, live, energies, precond):
    k, width = vectors.shape
    slots = tiles.shape[1] // width
    part = width // n_off
    owners = min(n_off, 2 * k // n)
    grow = 2 * k // (n * owners)
    outside = pl.BlockSpec(memory_space=pl.ANY)
    f32, b16 = jnp.float32, jnp.bfloat16
    vmem, dma = pltpu.VMEM, pltpu.SemaphoreType.DMA
    inside = pl.BlockSpec(memory_space=pltpu.VMEM)
    return pl.pallas_call(
        functools.partial(kernel, n, n_off, slots, float(width * n)),
        out_shape=(
            jax.ShapeDtypeStruct((k, width), f32),
            jax.ShapeDtypeStruct((k, k), f32),
        ),
        in_specs=[outside] * 5,
        out_specs=(inside, inside),
        scratch_shapes=[
            vmem((k, width), f32),
            pltpu.SMEM((1, slots), jnp.int32),
            vmem((1, width), f32),
            vmem((1, width), f32),
            vmem((k, part), f32),
            vmem((ITERS, slots, n_off, k, part), f32),
            vmem((slots, width, width), f32),
            vmem((slots, width, width), b16),
            vmem((slots, width, width), b16),
            vmem((k + 8, width), f32),
            vmem((slots, k + 8, width), f32),
            vmem((slots + 1, 2 * k, width), b16),
            vmem((ITERS, n_off, k, part), f32),
            vmem((ITERS, slots, n_off, k, part), f32),
            vmem((ITERS, n_off, slots + 1, k, part), f32),
            vmem((ITERS, k, part), f32),
            vmem((ITERS, k, width), f32),
            vmem((slots, k, width), f32),
            vmem((ITERS, n * owners, grow, 2 * k), f32),
            vmem((ITERS, n * n_off, grow, 2 * k), f32),
            vmem((ITERS, grow, 2 * k), f32),
            vmem((ITERS, n * owners, grow, 2 * k), f32),
            dma((slots + 4,)),
            dma((ITERS, slots, n_off)),
            dma((slots, n_off)),
            dma((slots, n_off)),
            dma((n_off * slots,)),
            dma((slots, n_off)),
            dma((ITERS, slots + 1, n_off)),
            dma((ITERS, n_off, slots + 1)),
            dma((n_off * slots,)),
            dma((slots, n_off)),
            dma((ITERS, n_off)),
            dma((ITERS, n_off)),
            dma((ITERS, n * owners)),
            dma((ITERS, n * n_off)),
            dma((ITERS, n * n_off)),
            dma((ITERS, n * owners)),
        ],
        compiler_params=pltpu.CompilerParams(
            collective_id=0, has_side_effects=True, vmem_limit_bytes=60 * 1024 * 1024
        ),
    )(vectors, tiles, live, energies[None, :], precond[None, :])


def solution(mesh):
    placed = (P(None, "row"), P("row", "off"), P("row", "off"), P("row"), P("row"))
    return jax.shard_map(
        functools.partial(local, mesh.shape["row"], mesh.shape["off"]),
        mesh=mesh, in_specs=placed, out_specs=(P(None, "row"), P()), check_vma=False,
    )
```

```python
import functools

import jax
import jax.numpy as jnp
from jax import lax
from jax.experimental import pallas as pl
from jax.experimental.pallas import tpu as pltpu
from jax.sharding import PartitionSpec as P

ITERS = 2
APPS = 3
GRANT = 60 * 1024 * 1024
MESH = pl.DeviceIdType.MESH
NN = (((1,), (0,)), ((), ()))
NT = (((1,), (1,)), ((), ()))


def coarse(left, right, dims):
    return lax.dot_general(left, right, dims, preferred_element_type=jnp.float32)


def halves(value):
    high = value.astype(jnp.bfloat16)
    low = (value - high.astype(jnp.float32)).astype(jnp.bfloat16)
    return high, low


def triple(left, right, dims=NN):
    left_hi, left_lo = halves(left)
    right_hi, right_lo = halves(right)
    count = left.shape[0]
    both = coarse(jnp.concatenate([left_hi, left_lo], axis=0), right_hi, dims)
    return both[:count] + both[count:] + coarse(left_hi, right_lo, dims)


def kernel(
    n, n_off, slots, total_rows,
    vec_hbm, tiles_ref, live_hbm, energy_hbm, precond_hbm,
    out_ref, ritz_ref,
    vec_ref, live_ref, energy_ref, precond_ref, acc, hand,
    raw, high, low, mine, near, split, direct, back, ret, part_a, own_a, near_a,
    gram, gram_in, gram_sum, gram_all,
    load_sem, hand_recv, fetch_relay, share_relay, fetch_send, fetch_recv, ret_send, ret_recv, share_send, share_recv,
    peer_send, peer_recv, gs_send, gs_recv, ga_send, ga_recv,
):
    me = lax.axis_index("row")
    off = lax.axis_index("off")
    k, width = vec_ref.shape
    part = width // n_off
    chunk = min(256, part)
    owners = min(n_off, 2 * k // n)
    grow = 2 * k // (n * owners)
    devices = n * n_off
    flat_me = me * n_off + off
    odd = lax.rem(me, 2) == 1
    small = devices <= 32

    def copy(src, dst, send, recv, row, col):
        return pltpu.make_async_remote_copy(
            src_ref=src, dst_ref=dst, send_sem=send, recv_sem=recv,
            device_id=(row, col), device_id_type=MESH,
        )

    def row_at(shift):
        return lax.rem(me + shift + n, n)

    def peer(step):
        return lax.rem(off + step, n_off)

    def cols(index):
        return pl.ds(pl.multiple_of(index * part, part), part)

    heads = [
        pltpu.make_async_copy(src, dst, load_sem.at[slots + index])
        for index, (src, dst) in enumerate(
            ((vec_hbm, vec_ref), (precond_hbm, precond_ref),
             (energy_hbm, energy_ref), (live_hbm, live_ref))
        )
    ]
    for one in heads:
        one.start()
    order = list(range(slots - 1, -1, -1))
    loads = [
        pltpu.make_async_copy(
            tiles_ref.at[:, pl.ds(slot * width, width)], raw.at[slot], load_sem.at[slot]
        )
        for slot in range(slots)
    ]
    for slot in order:
        loads[slot].start()

    barrier = pltpu.get_barrier_semaphore()

    def greet(step, carry):
        flat = lax.rem(flat_me + step, devices)
        pl.semaphore_signal(
            barrier, inc=1, device_id=(flat // n_off, lax.rem(flat, n_off)),
            device_id_type=MESH,
        )
        return carry

    lax.fori_loop(1, devices, greet, 0, unroll=small)
    for one in heads:
        one.wait()
    mine[:k, :] = vec_ref[...]
    mine[k:, :] = jnp.broadcast_to(precond_ref[...], (mine.shape[0] - k, width))
    pl.semaphore_wait(barrier, devices - 1)

    def spread(src, dst, send, recv, act):
        for group in range(n_off):
            for slot in range(slots):
                shift = group * slots + slot

                def step():
                    one = copy(
                        src, dst.at[slot, :, cols(off)], send.at[shift],
                        recv.at[slot, off], row_at(-shift), group,
                    )
                    act(one)

                if slot:
                    pl.when(lax.rem(me + shift, 2) == 1)(step)
                elif shift:
                    step()

    def relay(dst, send, recv, act):
        @pl.when(odd)
        def _():
            for slot in range(slots - 1):
                for q in range(n_off):
                    act(copy(
                        dst.at[slot, :, cols(q)], dst.at[slot + 1, :, cols(q)],
                        send.at[slot, q], recv.at[slot + 1, q], row_at(-1), off,
                    ))

    def begin(one):
        one.start()

    def finish(one):
        one.wait_send()

    def gathered(slot, dst, recv):
        for step in range(n_off):
            where = dst.at[slot, :, cols(step)]
            copy(where, where, recv.at[slot, step], recv.at[slot, step],
                 row_at(1), off).wait_recv()

    spread(mine.at[:, cols(off)], near, fetch_send, fetch_recv, begin)

    def put_split(where, value):
        hi, lo = halves(value)
        split[where, :k, :] = hi
        split[where, k:, :] = lo

    put_split(slots, vec_ref[...])

    def transposed(app, slot):
        for q in range(n_off):
            for c in range(part // chunk):
                at = pl.ds(q * part + c * chunk, chunk)
                both = coarse(split[slots], high[slot, :, at], NN)
                rest = coarse(split[slots, :k, :], low[slot, :, at], NN)
                back[app, slot, q, :, pl.ds(c * chunk, chunk)] = both[:k] + both[k:] + rest
            if slot:
                @pl.when(jnp.logical_not(odd))
                def _():
                    copy(
                        back.at[app, slot, q], hand.at[app, slot - 1, q],
                        ret_send.at[app, slot, q], hand_recv.at[app, slot - 1, q],
                        row_at(1), off,
                    ).start()

    def deliver(app, slot):
        shift = off * slots + slot
        for q in range(n_off):
            if slot < slots - 1:
                @pl.when(odd)
                def _():
                    where = hand.at[app, slot, q]
                    copy(where, where, hand_recv.at[app, slot, q],
                         hand_recv.at[app, slot, q], row_at(1), off).wait_recv()
                    back[app, slot, q] = back[app, slot, q] + hand[app, slot, q]

            def away():
                copy(
                    back.at[app, slot, q], ret.at[app, off, slot],
                    ret_send.at[app, slot, q], ret_recv.at[app, off, slot],
                    row_at(shift), q,
                ).start()

            pl.when(odd if slot else shift != 0)(away)

    def forward(it, slot, first):
        for c in range(width // chunk):
            at = pl.ds(c * chunk, chunk)
            both = coarse(split[slot], high[slot, at, :], NT)
            rest = coarse(split[slot, :k, :], low[slot, at, :], NT)
            term = both[:k] + both[k:] + rest
            q, place = (c * chunk) // part, (c * chunk) % part
            where = pl.ds(place, chunk)
            if first:
                direct[it, q, :, where] = term
            else:
                direct[it, q, :, where] = direct[it, q, :, where] + term

    rows = 32
    for slot in order:
        loads[slot].wait()
        limit = live_ref[0, slot]

        def cut(index, carry):
            start = pl.multiple_of(index * rows, rows)
            ids = lax.broadcasted_iota(jnp.int32, (rows, width), 0) + start
            value = jnp.where(ids < limit, raw[slot, pl.ds(start, rows), :], 0.0)
            hi, lo = halves(value)
            high[slot, pl.ds(start, rows), :] = hi
            low[slot, pl.ds(start, rows), :] = lo
            return carry

        lax.fori_loop(0, width // rows, cut, 0)
        transposed(0, slot)
        deliver(0, slot)

    def collect(dst, own, send, recv, use):
        for slot in range(slots):
            if slot == 0:
                @pl.when(off == 0)
                def _():
                    dst[0] = own[...]

                @pl.when(off != 0)
                def _():
                    gathered(0, dst, recv)
            else:
                gathered(slot, dst, recv)
            if slot == slots - 2:
                relay(dst, send, recv, begin)
            use(slot)

    def eye():
        return (
            lax.broadcasted_iota(jnp.int32, (k, k), 0)
            == lax.broadcasted_iota(jnp.int32, (k, k), 1)
        ).astype(jnp.float32)

    def exchange(app):
        @pl.when(off == 0)
        def _():
            for q in range(n_off):
                direct[app, q] = direct[app, q] + back[app, 0, q]

        for step in range(1, n_off):
            copy(
                direct.at[app, peer(step)], ret.at[app, off, slots],
                ret_send.at[app, slots, step], ret_recv.at[app, off, slots],
                me, peer(step),
            ).start()

    def image(app, value):
        acc[...] = energy_ref[:, cols(off)] * value + direct[app, off]
        for group in range(n_off):
            for slot in range(slots):
                def take():
                    where = ret.at[app, group, slot]
                    copy(where, where, ret_send.at[app, 0, 0], ret_recv.at[app, group, slot],
                         row_at(1), off).wait_recv()
                    acc[...] = acc[...] + ret[app, group, slot]

                if slot:
                    pl.when(lax.rem(me + group * slots + slot, 2) == 1)(take)
                elif group:
                    take()
        total = acc[...]
        for step in range(1, n_off):
            where = ret.at[app, peer(step), slots]
            copy(where, where, ret_send.at[app, 0, 0], ret_recv.at[app, peer(step), slots],
                 row_at(1), off).wait_recv()
            total = total + ret[app, peer(step), slots]
        return total

    def use_first(slot):
        put_split(slot, near[slot, :k, :])
        forward(0, slot, slot == 0)

    collect(near, mine, fetch_relay, fetch_recv, use_first)
    exchange(0)

    put_split(slots, precond_ref[...] * vec_ref[...])
    for slot in order:
        transposed(1, slot)
    for slot in range(slots):
        put_split(slot, near[slot, k : k + 1, :] * near[slot, :k, :])
        forward(1, slot, slot == 0)

    p_part = precond_ref[:, cols(off)]

    for it in range(ITERS):
        last = it == ITERS - 1
        if it == 0:
            x_part = vec_ref[:, cols(off)]
            total = image(0, x_part)
        else:
            x_part = out_ref[:, cols(off)]
            b_part = p_part * vec_ref[:, cols(off)]
            total_b = image(1, b_part)
            total_a = image(2, part_a[0])
            total = triple(both_fix, jnp.concatenate([total_a, total_b], axis=0))
        a_part = x_part - p_part * total
        part_a[it] = a_part
        own_a[it, :, cols(off)] = a_part
        for step in range(1, n_off):
            copy(
                part_a.at[it], own_a.at[it, :, cols(off)],
                peer_send.at[it, step], peer_recv.at[it, off], me, peer(step),
            ).start()
        if not last:
            spread(part_a.at[it], near_a, share_send, share_recv, begin)
            for slot in order:
                deliver(1, slot)
            exchange(1)

        ab = jnp.concatenate([a_part, p_part * x_part], axis=0)
        inner = triple(ab, ab, NT)
        xy = triple(x_part, total, NT)
        low_half = jnp.concatenate([xy, inner[k:, k:]], axis=1)
        packed = jnp.concatenate([inner[:k, :], low_half], axis=0)
        for t in range(n * owners):
            gram[it, t] = packed[t * grow : (t + 1) * grow, :]

        def owner_at(step):
            index = lax.rem(me * owners + lax.rem(off, owners) + step, n * owners)
            return index, index // owners, lax.rem(index, owners)

        def deal(step, carry):
            index, row, col = owner_at(step)
            copy(
                gram.at[it, index], gram_in.at[it, flat_me], gs_send.at[it, index],
                gs_recv.at[it, flat_me], row, col,
            ).start()
            return carry

        def add(step, piece):
            source = lax.rem(flat_me + step, devices)
            where = gram_in.at[it, source]
            copy(where, where, gs_send.at[it, 0], gs_recv.at[it, source],
                 row_at(1), off).wait_recv()
            return piece + gram_in[it, source]

        def tell(step, carry):
            target = lax.rem(flat_me + step, devices)
            copy(
                gram_sum.at[it], gram_all.at[it, me * owners + off], ga_send.at[it, target],
                ga_recv.at[it, me * owners + off], target // n_off, lax.rem(target, n_off),
            ).start()
            return carry

        def hear(step, carry):
            index = owner_at(step)[0]
            where = gram_all.at[it, index]
            copy(where, where, ga_send.at[it, 0], ga_recv.at[it, index],
                 row_at(1), off).wait_recv()
            return carry

        def own():
            piece = lax.fori_loop(
                1, devices, add, gram[it, me * owners + off], unroll=small
            )
            gram_sum[it] = piece
            gram_all[it, me * owners + off] = piece
            lax.fori_loop(1, devices, tell, 0, unroll=small)

        lax.fori_loop(1, n * owners, deal, 0, unroll=small)
        for step in range(1, n_off):
            where = own_a.at[it, :, cols(peer(step))]
            copy(where, where, peer_send.at[it, step], peer_recv.at[it, peer(step)],
                 row_at(1), off).wait_recv()
        if not last:
            put_split(slots, own_a[0])
            for slot in order:
                transposed(2, slot)
                deliver(2, slot)
        if owners == n_off:
            own()
        else:
            pl.when(off < owners)(own)

            @pl.when(off >= owners)
            def _():
                deal(0, 0)
                hear(0, 0)

        if not last:
            def use_second(slot):
                put_split(slot, near_a[slot])
                forward(2, slot, slot == 0)

            collect(near_a, own_a.at[0], share_relay, share_recv, use_second)
            exchange(2)
        lax.fori_loop(1, n * owners, hear, 0, unroll=small)
        full = gram_all[it].reshape(2 * k, 2 * k) / total_rows
        turned = full.T
        ritz, ritz_t = full[k:, :k], turned[:k, k:]
        aa, cross, cross_t, bb = full[:k, :k], full[:k, k:], turned[k:, :k], full[k:, k:]
        mixed = triple(jnp.concatenate([cross, bb], axis=0), ritz)
        overlap = aa + mixed[:k] + triple(ritz_t, cross_t + mixed[k:])
        fix = 1.5 * eye() - 0.5 * overlap
        both_fix = jnp.concatenate([fix, triple(fix, ritz_t)], axis=1)

        state = vec_ref if it == 0 else out_ref
        out_ref[...] = triple(
            both_fix,
            jnp.concatenate([own_a[it], precond_ref[...] * state[...]], axis=0),
        )
        if last:
            ritz_ref[...] = ritz

    spread(mine.at[:, cols(off)], near, fetch_send, fetch_recv, finish)
    relay(near, fetch_relay, fetch_recv, finish)
    spread(part_a.at[0], near_a, share_send, share_recv, finish)
    relay(near_a, share_relay, share_recv, finish)
    for app in range(APPS):
        for slot in range(slots):
            for q in range(n_off):
                def gone():
                    copy(back.at[app, slot, q], ret.at[app, off, slot],
                         ret_send.at[app, slot, q], ret_recv.at[app, off, slot],
                         row_at(1), q).wait_send()

                if slot:
                    gone()
                else:
                    pl.when(off != 0)(gone)
        for step in range(1, n_off):
            copy(direct.at[app, 0], ret.at[app, off, slots], ret_send.at[app, slots, step],
                 ret_recv.at[app, off, slots], me, peer(step)).wait_send()
    for it in range(ITERS):
        for step in range(1, n_off):
            copy(part_a.at[it], part_a.at[it], peer_send.at[it, step],
                 peer_recv.at[it, off], me, peer(step)).wait_send()

        def dealt(step, carry):
            index = lax.rem(me * owners + lax.rem(off, owners) + step, n * owners)
            copy(gram_sum.at[it], gram_sum.at[it], gs_send.at[it, index],
                 gs_recv.at[it, 0], row_at(1), off).wait_send()
            return carry

        def told(step, carry):
            target = lax.rem(flat_me + step, devices)
            copy(gram_sum.at[it], gram_sum.at[it], ga_send.at[it, target],
                 ga_recv.at[it, 0], row_at(1), off).wait_send()
            return carry

        lax.fori_loop(1, n * owners, dealt, 0, unroll=small)
        if owners == n_off:
            lax.fori_loop(1, devices, told, 0, unroll=small)
        else:
            @pl.when(off < owners)
            def _():
                lax.fori_loop(1, devices, told, 0)

            @pl.when(off >= owners)
            def _():
                dealt(0, 0)


def hand_over(basis_in, ritz_in, basis_out, ritz_out, sems):
    moves = [
        pltpu.make_async_copy(basis_in, basis_out, sems.at[0]),
        pltpu.make_async_copy(ritz_in, ritz_out, sems.at[1]),
    ]
    for one in moves:
        one.start()
    for one in moves:
        one.wait()


def local(n, n_off, vectors, tiles, live, energies, precond):
    k, width = vectors.shape
    slots = tiles.shape[1] // width
    part = width // n_off
    owners = min(n_off, 2 * k // n)
    grow = 2 * k // (n * owners)
    outside = pl.BlockSpec(memory_space=pl.ANY)
    f32, b16 = jnp.float32, jnp.bfloat16
    vmem, dma = pltpu.VMEM, pltpu.SemaphoreType.DMA
    inside = pl.BlockSpec(memory_space=pltpu.VMEM)
    basis, ritz = pl.pallas_call(
        functools.partial(kernel, n, n_off, slots, float(width * n)),
        out_shape=(
            jax.ShapeDtypeStruct((k, width), f32),
            jax.ShapeDtypeStruct((k, k), f32),
        ),
        in_specs=[outside] * 5,
        out_specs=(inside, inside),
        scratch_shapes=[
            vmem((k, width), f32),
            pltpu.SMEM((1, slots), jnp.int32),
            vmem((1, width), f32),
            vmem((1, width), f32),
            vmem((k, part), f32),
            vmem((APPS, slots, n_off, k, part), f32),
            vmem((slots, width, width), f32),
            vmem((slots, width, width), b16),
            vmem((slots, width, width), b16),
            vmem((k + 8, width), f32),
            vmem((slots, k + 8, width), f32),
            vmem((slots + 1, 2 * k, width), b16),
            vmem((APPS, n_off, k, part), f32),
            vmem((APPS, slots, n_off, k, part), f32),
            vmem((APPS, n_off, slots + 1, k, part), f32),
            vmem((ITERS, k, part), f32),
            vmem((ITERS, k, width), f32),
            vmem((slots, k, width), f32),
            vmem((ITERS, n * owners, grow, 2 * k), f32),
            vmem((ITERS, n * n_off, grow, 2 * k), f32),
            vmem((ITERS, grow, 2 * k), f32),
            vmem((ITERS, n * owners, grow, 2 * k), f32),
            dma((slots + 4,)),
            dma((APPS, slots, n_off)),
            dma((slots, n_off)),
            dma((slots, n_off)),
            dma((n_off * slots,)),
            dma((slots, n_off)),
            dma((APPS, slots + 1, n_off)),
            dma((APPS, n_off, slots + 1)),
            dma((n_off * slots,)),
            dma((slots, n_off)),
            dma((ITERS, n_off)),
            dma((ITERS, n_off)),
            dma((ITERS, n * owners)),
            dma((ITERS, n * n_off)),
            dma((ITERS, n * n_off)),
            dma((ITERS, n * owners)),
        ],
        compiler_params=pltpu.CompilerParams(
            collective_id=0, has_side_effects=True, vmem_limit_bytes=GRANT
        ),
    )(vectors, tiles, live, energies[None, :], precond[None, :])
    return pl.pallas_call(
        hand_over,
        out_shape=(
            jax.ShapeDtypeStruct((k, width), f32),
            jax.ShapeDtypeStruct((k, k), f32),
        ),
        in_specs=[outside] * 2,
        out_specs=(outside, outside),
        scratch_shapes=[dma((2,))],
        compiler_params=pltpu.CompilerParams(vmem_limit_bytes=GRANT),
    )(basis, ritz)


def solution(mesh):
    placed = (P(None, "row"), P("row", "off"), P("row", "off"), P("row"), P("row"))
    return jax.shard_map(
        functools.partial(local, mesh.shape["row"], mesh.shape["off"]),
        mesh=mesh, in_specs=placed, out_specs=(P(None, "row"), P()), check_vma=False,
    )
```

```python
import functools

import jax
import jax.numpy as jnp
from jax import lax
from jax.experimental import pallas as pl
from jax.experimental.pallas import tpu as pltpu
from jax.sharding import PartitionSpec as P

ITERS = 2
APPS = 3
GRANT = 60 * 1024 * 1024
MESH = pl.DeviceIdType.MESH
NN = (((1,), (0,)), ((), ()))
NT = (((1,), (1,)), ((), ()))


def coarse(left, right, dims):
    return lax.dot_general(left, right, dims, preferred_element_type=jnp.float32)


def halves(value):
    high = value.astype(jnp.bfloat16)
    low = (value - high.astype(jnp.float32)).astype(jnp.bfloat16)
    return high, low


def triple(left, right, dims=NN):
    left_hi, left_lo = halves(left)
    right_hi, right_lo = halves(right)
    count = left.shape[0]
    both = coarse(jnp.concatenate([left_hi, left_lo], axis=0), right_hi, dims)
    return both[:count] + both[count:] + coarse(left_hi, right_lo, dims)


def shares(n, n_off, k):
    block = 4 if n % 4 == 0 else 1
    while 2 * k % (block * n_off):
        block //= 2
    team = block * n_off
    return block, team, n // block, 2 * k // team


def kernel(
    n, n_off, slots, total_rows,
    vec_hbm, tiles_ref, live_hbm, energy_hbm, precond_hbm,
    out_ref, ritz_ref,
    vec_ref, live_ref, energy_ref, precond_ref, acc, hand,
    raw, high, low, mine, near, split, direct, back, ret, part_a, own_a, near_a,
    gram, gram_in, gram_off, gram_sum, gram_all,
    load_sem, hand_recv, fetch_relay, share_relay, fetch_send, fetch_recv, ret_send, ret_recv, share_send, share_recv,
    peer_send, peer_recv, gs_send, gs_recv, go_send, go_recv, ga_send, ga_recv,
):
    me = lax.axis_index("row")
    off = lax.axis_index("off")
    k, width = vec_ref.shape
    part = width // n_off
    chunk = min(256, part)
    block, team, floors, grow = shares(n, n_off, k)
    floor, base = me // block, me - lax.rem(me, block)
    spot = lax.rem(me, block) * n_off + off
    devices = n * n_off
    flat_me = me * n_off + off
    odd = lax.rem(me, 2) == 1
    small = devices <= 32

    def copy(src, dst, send, recv, row, col):
        return pltpu.make_async_remote_copy(
            src_ref=src, dst_ref=dst, send_sem=send, recv_sem=recv,
            device_id=(row, col), device_id_type=MESH,
        )

    def row_at(shift):
        return lax.rem(me + shift + n, n)

    def peer(step):
        return lax.rem(off + step, n_off)

    def cols(index):
        return pl.ds(pl.multiple_of(index * part, part), part)

    heads = [
        pltpu.make_async_copy(src, dst, load_sem.at[slots + index])
        for index, (src, dst) in enumerate(
            ((vec_hbm, vec_ref), (precond_hbm, precond_ref),
             (energy_hbm, energy_ref), (live_hbm, live_ref))
        )
    ]
    for one in heads:
        one.start()
    order = list(range(slots - 1, -1, -1))
    loads = [
        pltpu.make_async_copy(
            tiles_ref.at[:, pl.ds(slot * width, width)], raw.at[slot], load_sem.at[slot]
        )
        for slot in range(slots)
    ]
    for slot in order:
        loads[slot].start()

    barrier = pltpu.get_barrier_semaphore()

    def greet(step, carry):
        flat = lax.rem(flat_me + step, devices)
        pl.semaphore_signal(
            barrier, inc=1, device_id=(flat // n_off, lax.rem(flat, n_off)),
            device_id_type=MESH,
        )
        return carry

    lax.fori_loop(1, devices, greet, 0, unroll=small)
    for one in heads:
        one.wait()
    mine[:k, :] = vec_ref[...]
    mine[k:, :] = jnp.broadcast_to(precond_ref[...], (mine.shape[0] - k, width))
    pl.semaphore_wait(barrier, devices - 1)

    def spread(src, dst, send, recv, act):
        for group in range(n_off):
            for slot in range(slots):
                shift = group * slots + slot

                def step():
                    one = copy(
                        src, dst.at[slot, :, cols(off)], send.at[shift],
                        recv.at[slot, off], row_at(-shift), group,
                    )
                    act(one)

                if slot:
                    pl.when(lax.rem(me + shift, 2) == 1)(step)
                elif shift:
                    step()

    def relay(dst, send, recv, act):
        @pl.when(odd)
        def _():
            for slot in range(slots - 1):
                for q in range(n_off):
                    act(copy(
                        dst.at[slot, :, cols(q)], dst.at[slot + 1, :, cols(q)],
                        send.at[slot, q], recv.at[slot + 1, q], row_at(-1), off,
                    ))

    def begin(one):
        one.start()

    def finish(one):
        one.wait_send()

    def gathered(slot, dst, recv):
        for step in range(n_off):
            where = dst.at[slot, :, cols(step)]
            copy(where, where, recv.at[slot, step], recv.at[slot, step],
                 row_at(1), off).wait_recv()

    spread(mine.at[:, cols(off)], near, fetch_send, fetch_recv, begin)

    def put_split(where, value):
        count = value.shape[0]
        hi, lo = halves(value)
        split[where, :count, :] = hi
        split[where, count : 2 * count, :] = lo

    def pair(value, p_row):
        return jnp.concatenate([value, p_row * value], axis=0)

    put_split(slots, pair(vec_ref[...], precond_ref[...]))

    def transposed(apps, slot):
        count = k * len(apps)
        for q in range(n_off):
            for c in range(part // chunk):
                at = pl.ds(q * part + c * chunk, chunk)
                both = coarse(split[slots, : 2 * count, :], high[slot, :, at], NN)
                rest = coarse(split[slots, :count, :], low[slot, :, at], NN)
                term = both[:count] + both[count:] + rest
                for index, app in enumerate(apps):
                    back[app, slot, q, :, pl.ds(c * chunk, chunk)] = (
                        term[index * k : (index + 1) * k]
                    )
            for app in apps:
                hand_on(app, slot, q)

    def hand_on(app, slot, q):
        if slot:
            @pl.when(jnp.logical_not(odd))
            def _():
                copy(
                    back.at[app, slot, q], hand.at[app, slot - 1, q],
                    ret_send.at[app, slot, q], hand_recv.at[app, slot - 1, q],
                    row_at(1), off,
                ).start()

    def deliver(app, slot):
        shift = off * slots + slot
        for q in range(n_off):
            if slot < slots - 1:
                @pl.when(odd)
                def _():
                    where = hand.at[app, slot, q]
                    copy(where, where, hand_recv.at[app, slot, q],
                         hand_recv.at[app, slot, q], row_at(1), off).wait_recv()
                    back[app, slot, q] = back[app, slot, q] + hand[app, slot, q]

            def away():
                copy(
                    back.at[app, slot, q], ret.at[app, off, slot],
                    ret_send.at[app, slot, q], ret_recv.at[app, off, slot],
                    row_at(shift), q,
                ).start()

            pl.when(odd if slot else shift != 0)(away)

    def forward(apps, slot, first):
        count = k * len(apps)
        for c in range(width // chunk):
            at = pl.ds(c * chunk, chunk)
            both = coarse(split[slot, : 2 * count, :], high[slot, at, :], NT)
            rest = coarse(split[slot, :count, :], low[slot, at, :], NT)
            term = both[:count] + both[count:] + rest
            q, place = (c * chunk) // part, (c * chunk) % part
            where = pl.ds(place, chunk)
            for index, app in enumerate(apps):
                one = term[index * k : (index + 1) * k]
                if first:
                    direct[app, q, :, where] = one
                else:
                    direct[app, q, :, where] = direct[app, q, :, where] + one

    rows = 32
    for slot in order:
        loads[slot].wait()
        limit = live_ref[0, slot]

        def cut(index, carry):
            start = pl.multiple_of(index * rows, rows)
            ids = lax.broadcasted_iota(jnp.int32, (rows, width), 0) + start
            value = jnp.where(ids < limit, raw[slot, pl.ds(start, rows), :], 0.0)
            hi, lo = halves(value)
            high[slot, pl.ds(start, rows), :] = hi
            low[slot, pl.ds(start, rows), :] = lo
            return carry

        lax.fori_loop(0, width // rows, cut, 0)
        transposed((0, 1), slot)
        deliver(0, slot)

    def collect(dst, own, send, recv, use):
        for slot in range(slots):
            if slot == 0:
                @pl.when(off == 0)
                def _():
                    dst[0] = own[...]

                @pl.when(off != 0)
                def _():
                    gathered(0, dst, recv)
            else:
                gathered(slot, dst, recv)
            if slot == slots - 2:
                relay(dst, send, recv, begin)
            use(slot)

    def eye():
        return (
            lax.broadcasted_iota(jnp.int32, (k, k), 0)
            == lax.broadcasted_iota(jnp.int32, (k, k), 1)
        ).astype(jnp.float32)

    def exchange(app):
        @pl.when(off == 0)
        def _():
            for q in range(n_off):
                direct[app, q] = direct[app, q] + back[app, 0, q]

        for step in range(1, n_off):
            copy(
                direct.at[app, peer(step)], ret.at[app, off, slots],
                ret_send.at[app, slots, step], ret_recv.at[app, off, slots],
                me, peer(step),
            ).start()

    def image(app, value):
        acc[...] = energy_ref[:, cols(off)] * value + direct[app, off]
        for group in range(n_off):
            for slot in range(slots):
                def take():
                    where = ret.at[app, group, slot]
                    copy(where, where, ret_send.at[app, 0, 0], ret_recv.at[app, group, slot],
                         row_at(1), off).wait_recv()
                    acc[...] = acc[...] + ret[app, group, slot]

                if slot:
                    pl.when(lax.rem(me + group * slots + slot, 2) == 1)(take)
                elif group:
                    take()
        total = acc[...]
        for step in range(1, n_off):
            where = ret.at[app, peer(step), slots]
            copy(where, where, ret_send.at[app, 0, 0], ret_recv.at[app, peer(step), slots],
                 row_at(1), off).wait_recv()
            total = total + ret[app, peer(step), slots]
        return total

    def use_first(slot):
        put_split(slot, pair(near[slot, :k, :], near[slot, k : k + 1, :]))
        forward((0, 1), slot, slot == 0)

    collect(near, mine, fetch_relay, fetch_recv, use_first)
    exchange(0)

    p_part = precond_ref[:, cols(off)]

    for it in range(ITERS):
        last = it == ITERS - 1
        if it == 0:
            x_part = vec_ref[:, cols(off)]
            total = image(0, x_part)
        else:
            x_part = out_ref[:, cols(off)]
            b_part = p_part * vec_ref[:, cols(off)]
            total_b = image(1, b_part)
            total_a = image(2, part_a[0])
            total = triple(both_fix, jnp.concatenate([total_a, total_b], axis=0))
        a_part = x_part - p_part * total
        part_a[it] = a_part
        own_a[it, :, cols(off)] = a_part
        for step in range(1, n_off):
            copy(
                part_a.at[it], own_a.at[it, :, cols(off)],
                peer_send.at[it, step], peer_recv.at[it, off], me, peer(step),
            ).start()
        if not last:
            spread(part_a.at[it], near_a, share_send, share_recv, begin)
            for slot in order:
                deliver(1, slot)
            exchange(1)

        ab = jnp.concatenate([a_part, p_part * x_part], axis=0)
        inner = triple(ab, ab, NT)
        xy = triple(x_part, total, NT)
        low_half = jnp.concatenate([xy, inner[k:, k:]], axis=1)
        packed = jnp.concatenate([inner[:k, :], low_half], axis=0)
        for t in range(team):
            gram[it, t] = packed[t * grow : (t + 1) * grow, :]

        def mate(step):
            index = lax.rem(spot + step, team)
            return index, base + index // n_off, lax.rem(index, n_off)

        for step in range(1, team):
            index, row, col = mate(step)
            copy(
                gram.at[it, index], gram_in.at[it, spot], gs_send.at[it, step],
                gs_recv.at[it, spot], row, col,
            ).start()
        for step in range(1, n_off):
            where = own_a.at[it, :, cols(peer(step))]
            copy(where, where, peer_send.at[it, step], peer_recv.at[it, peer(step)],
                 row_at(1), off).wait_recv()
        if not last:
            put_split(slots, own_a[0])
            for slot in order:
                transposed((2,), slot)
                deliver(2, slot)
        piece = gram[it, spot]
        for step in range(1, team):
            index = mate(step)[0]
            where = gram_in.at[it, index]
            copy(where, where, gs_send.at[it, step], gs_recv.at[it, index],
                 row_at(1), off).wait_recv()
            piece = piece + gram_in[it, index]
        gram_off[it, floor] = piece
        for step in range(1, floors):
            copy(
                gram_off.at[it, floor], gram_off.at[it, floor], go_send.at[it, step],
                go_recv.at[it, floor], row_at(step * block), off,
            ).start()

        for step in range(1, floors):
            index = lax.rem(floor + step, floors)
            where = gram_off.at[it, index]
            copy(where, where, go_send.at[it, step], go_recv.at[it, index],
                 row_at(1), off).wait_recv()
        piece = gram_off[it, 0]
        for index in range(1, floors):
            piece = piece + gram_off[it, index]
        gram_sum[it] = piece
        gram_all[it, spot] = piece
        for step in range(1, team):
            index, row, col = mate(step)
            copy(
                gram_sum.at[it], gram_all.at[it, spot], ga_send.at[it, step],
                ga_recv.at[it, spot], row, col,
            ).start()
        if not last:
            def use_second(slot):
                put_split(slot, near_a[slot])
                forward((2,), slot, slot == 0)

            collect(near_a, own_a.at[0], share_relay, share_recv, use_second)
            exchange(2)
        for step in range(1, team):
            index = mate(step)[0]
            where = gram_all.at[it, index]
            copy(where, where, ga_send.at[it, step], ga_recv.at[it, index],
                 row_at(1), off).wait_recv()
        full = gram_all[it].reshape(2 * k, 2 * k) / total_rows
        turned = full.T
        ritz, ritz_t = full[k:, :k], turned[:k, k:]
        aa, cross, cross_t, bb = full[:k, :k], full[:k, k:], turned[k:, :k], full[k:, k:]
        mixed = triple(jnp.concatenate([cross, bb], axis=0), ritz)
        overlap = aa + mixed[:k] + triple(ritz_t, cross_t + mixed[k:])
        fix = 1.5 * eye() - 0.5 * overlap
        both_fix = jnp.concatenate([fix, triple(fix, ritz_t)], axis=1)

        state = vec_ref if it == 0 else out_ref
        out_ref[...] = triple(
            both_fix,
            jnp.concatenate([own_a[it], precond_ref[...] * state[...]], axis=0),
        )
        if last:
            ritz_ref[...] = ritz

    spread(mine.at[:, cols(off)], near, fetch_send, fetch_recv, finish)
    relay(near, fetch_relay, fetch_recv, finish)
    spread(part_a.at[0], near_a, share_send, share_recv, finish)
    relay(near_a, share_relay, share_recv, finish)
    for app in range(APPS):
        for slot in range(slots):
            for q in range(n_off):
                def gone():
                    copy(back.at[app, slot, q], ret.at[app, off, slot],
                         ret_send.at[app, slot, q], ret_recv.at[app, off, slot],
                         row_at(1), q).wait_send()

                if slot:
                    gone()
                else:
                    pl.when(off != 0)(gone)
        for step in range(1, n_off):
            copy(direct.at[app, 0], ret.at[app, off, slots], ret_send.at[app, slots, step],
                 ret_recv.at[app, off, slots], me, peer(step)).wait_send()
    for it in range(ITERS):
        for step in range(1, n_off):
            copy(part_a.at[it], part_a.at[it], peer_send.at[it, step],
                 peer_recv.at[it, off], me, peer(step)).wait_send()

        for step in range(1, team):
            copy(gram_sum.at[it], gram_sum.at[it], gs_send.at[it, step],
                 gs_recv.at[it, 0], row_at(1), off).wait_send()
            copy(gram_sum.at[it], gram_sum.at[it], ga_send.at[it, step],
                 ga_recv.at[it, 0], row_at(1), off).wait_send()
        for step in range(1, floors):
            copy(gram_sum.at[it], gram_sum.at[it], go_send.at[it, step],
                 go_recv.at[it, 0], row_at(1), off).wait_send()


def hand_over(basis_in, ritz_in, basis_out, ritz_out, sems):
    moves = [
        pltpu.make_async_copy(basis_in, basis_out, sems.at[0]),
        pltpu.make_async_copy(ritz_in, ritz_out, sems.at[1]),
    ]
    for one in moves:
        one.start()
    for one in moves:
        one.wait()


def local(n, n_off, vectors, tiles, live, energies, precond):
    k, width = vectors.shape
    slots = tiles.shape[1] // width
    part = width // n_off
    _, team, floors, grow = shares(n, n_off, k)
    outside = pl.BlockSpec(memory_space=pltpu.HBM)
    f32, b16 = jnp.float32, jnp.bfloat16
    vmem, dma = pltpu.VMEM, pltpu.SemaphoreType.DMA
    inside = pl.BlockSpec(memory_space=pltpu.VMEM)
    basis, ritz = pl.pallas_call(
        functools.partial(kernel, n, n_off, slots, float(width * n)),
        out_shape=(
            jax.ShapeDtypeStruct((k, width), f32),
            jax.ShapeDtypeStruct((k, k), f32),
        ),
        in_specs=[outside] * 5,
        out_specs=(inside, inside),
        scratch_shapes=[
            vmem((k, width), f32),
            pltpu.SMEM((1, slots), jnp.int32),
            vmem((1, width), f32),
            vmem((1, width), f32),
            vmem((k, part), f32),
            vmem((APPS, slots, n_off, k, part), f32),
            vmem((slots, width, width), f32),
            vmem((slots, width, width), b16),
            vmem((slots, width, width), b16),
            vmem((k + 8, width), f32),
            vmem((slots, k + 8, width), f32),
            vmem((slots + 1, 4 * k, width), b16),
            vmem((APPS, n_off, k, part), f32),
            vmem((APPS, slots, n_off, k, part), f32),
            vmem((APPS, n_off, slots + 1, k, part), f32),
            vmem((ITERS, k, part), f32),
            vmem((ITERS, k, width), f32),
            vmem((slots, k, width), f32),
            vmem((ITERS, team, grow, 2 * k), f32),
            vmem((ITERS, team, grow, 2 * k), f32),
            vmem((ITERS, floors, grow, 2 * k), f32),
            vmem((ITERS, grow, 2 * k), f32),
            vmem((ITERS, team, grow, 2 * k), f32),
            dma((slots + 4,)),
            dma((APPS, slots, n_off)),
            dma((slots, n_off)),
            dma((slots, n_off)),
            dma((n_off * slots,)),
            dma((slots, n_off)),
            dma((APPS, slots + 1, n_off)),
            dma((APPS, n_off, slots + 1)),
            dma((n_off * slots,)),
            dma((slots, n_off)),
            dma((ITERS, n_off)),
            dma((ITERS, n_off)),
            dma((ITERS, team)),
            dma((ITERS, team)),
            dma((ITERS, floors)),
            dma((ITERS, floors)),
            dma((ITERS, team)),
            dma((ITERS, team)),
        ],
        compiler_params=pltpu.CompilerParams(
            collective_id=0, has_side_effects=True, vmem_limit_bytes=GRANT
        ),
    )(vectors, tiles, live, energies[None, :], precond[None, :])
    return pl.pallas_call(
        hand_over,
        out_shape=(
            jax.ShapeDtypeStruct((k, width), f32),
            jax.ShapeDtypeStruct((k, k), f32),
        ),
        in_specs=[inside] * 2,
        out_specs=(outside, outside),
        scratch_shapes=[dma((2,))],
        compiler_params=pltpu.CompilerParams(vmem_limit_bytes=GRANT),
    )(basis, ritz)


def solution(mesh):
    placed = (P(None, "row"), P("row", "off"), P("row", "off"), P("row"), P("row"))
    return jax.shard_map(
        functools.partial(local, mesh.shape["row"], mesh.shape["off"]),
        mesh=mesh, in_specs=placed, out_specs=(P(None, "row"), P()), check_vma=False,
    )
```

```python
import functools

import jax
import jax.numpy as jnp
from jax import lax
from jax.experimental import pallas as pl
from jax.experimental.pallas import tpu as pltpu
from jax.sharding import PartitionSpec as P

ITERS = 2
APPS = 3
SPAN = 128
GRANT = 60 * 1024 * 1024
MESH = pl.DeviceIdType.MESH
NN = (((1,), (0,)), ((), ()))
NT = (((1,), (1,)), ((), ()))


def coarse(left, right, dims):
    return lax.dot_general(left, right, dims, preferred_element_type=jnp.float32)


def halves(value):
    high = value.astype(jnp.bfloat16)
    low = (value - high.astype(jnp.float32)).astype(jnp.bfloat16)
    return high, low


def triple(left, right, dims=NN):
    left_hi, left_lo = halves(left)
    right_hi, right_lo = halves(right)
    count = left.shape[0]
    both = coarse(jnp.concatenate([left_hi, left_lo], axis=0), right_hi, dims)
    return both[:count] + both[count:] + coarse(left_hi, right_lo, dims)


def shares(n, n_off, k):
    block = 4 if n % 4 == 0 else 1
    while 2 * k % (block * n_off):
        block //= 2
    team = block * n_off
    return block, team, n // block, 2 * k // team


def kernel(
    n, n_off, slots, total_rows,
    vec_hbm, tiles_ref, live_hbm, energy_hbm, precond_hbm,
    out_ref, ritz_ref,
    vec_ref, live_ref, energy_ref, precond_ref, acc, hand,
    raw, high, low, mine, near, split, direct, back, ret, part_a, own_a, near_a,
    gram, gram_in, gram_off, gram_sum, gram_all,
    load_sem, tile_sem, hand_recv, fetch_relay, share_relay, fetch_send, fetch_recv, ret_send, ret_recv, share_send, share_recv,
    peer_send, peer_recv, gs_send, gs_recv, go_send, go_recv, ga_send, ga_recv,
):
    me = lax.axis_index("row")
    off = lax.axis_index("off")
    k, width = vec_ref.shape
    part = width // n_off
    chunk = min(256, part)
    block, team, floors, grow = shares(n, n_off, k)
    floor, base = me // block, me - lax.rem(me, block)
    spot = lax.rem(me, block) * n_off + off
    devices = n * n_off
    flat_me = me * n_off + off
    odd = lax.rem(me, 2) == 1
    small = devices <= 32

    def copy(src, dst, send, recv, row, col):
        return pltpu.make_async_remote_copy(
            src_ref=src, dst_ref=dst, send_sem=send, recv_sem=recv,
            device_id=(row, col), device_id_type=MESH,
        )

    def row_at(shift):
        return lax.rem(me + shift + n, n)

    def peer(step):
        return lax.rem(off + step, n_off)

    def cols(index):
        return pl.ds(pl.multiple_of(index * part, part), part)

    heads = [
        pltpu.make_async_copy(src, dst, load_sem.at[slots + index])
        for index, (src, dst) in enumerate(
            ((vec_hbm, vec_ref), (precond_hbm, precond_ref),
             (energy_hbm, energy_ref), (live_hbm, live_ref))
        )
    ]
    for one in heads:
        one.start()
    order = list(range(slots - 1, -1, -1))
    span = SPAN
    loads = [
        [
            pltpu.make_async_copy(
                tiles_ref.at[pl.ds(piece * span, span), pl.ds(slot * width, width)],
                raw.at[slot, pl.ds(piece * span, span), :], tile_sem.at[slot, piece],
            )
            for piece in range(width // span)
        ]
        for slot in range(slots)
    ]
    for slot in order:
        for one in loads[slot]:
            one.start()

    barrier = pltpu.get_barrier_semaphore()

    def greet(step, carry):
        flat = lax.rem(flat_me + step, devices)
        pl.semaphore_signal(
            barrier, inc=1, device_id=(flat // n_off, lax.rem(flat, n_off)),
            device_id_type=MESH,
        )
        return carry

    lax.fori_loop(1, devices, greet, 0, unroll=small)
    for one in heads:
        one.wait()
    mine[:k, :] = vec_ref[...]
    mine[k:, :] = jnp.broadcast_to(precond_ref[...], (mine.shape[0] - k, width))
    pl.semaphore_wait(barrier, devices - 1)

    def spread(src, dst, send, recv, act):
        for group in range(n_off):
            for slot in range(slots):
                shift = group * slots + slot

                def step():
                    one = copy(
                        src, dst.at[slot, :, cols(off)], send.at[shift],
                        recv.at[slot, off], row_at(-shift), group,
                    )
                    act(one)

                if slot:
                    pl.when(lax.rem(me + shift, 2) == 1)(step)
                elif shift:
                    step()

    def relay(dst, send, recv, act):
        @pl.when(odd)
        def _():
            for slot in range(slots - 1):
                for q in range(n_off):
                    act(copy(
                        dst.at[slot, :, cols(q)], dst.at[slot + 1, :, cols(q)],
                        send.at[slot, q], recv.at[slot + 1, q], row_at(-1), off,
                    ))

    def begin(one):
        one.start()

    def finish(one):
        one.wait_send()

    def gathered(slot, dst, recv):
        for step in range(n_off):
            where = dst.at[slot, :, cols(step)]
            copy(where, where, recv.at[slot, step], recv.at[slot, step],
                 row_at(1), off).wait_recv()

    spread(mine.at[:, cols(off)], near, fetch_send, fetch_recv, begin)

    def put_split(where, value):
        count = value.shape[0]
        hi, lo = halves(value)
        split[where, :count, :] = hi
        split[where, count : 2 * count, :] = lo

    put_split(slots, vec_ref[...])

    def transposed(apps, slot):
        count = k * len(apps)
        for q in range(n_off):
            for c in range(part // chunk):
                at = pl.ds(q * part + c * chunk, chunk)
                both = coarse(split[slots, : 2 * count, :], high[slot, :, at], NN)
                rest = coarse(split[slots, :count, :], low[slot, :, at], NN)
                term = both[:count] + both[count:] + rest
                for index, app in enumerate(apps):
                    back[app, slot, q, :, pl.ds(c * chunk, chunk)] = (
                        term[index * k : (index + 1) * k]
                    )
            for app in apps:
                hand_on(app, slot, q)

    def hand_on(app, slot, q):
        if slot:
            @pl.when(jnp.logical_not(odd))
            def _():
                copy(
                    back.at[app, slot, q], hand.at[app, slot - 1, q],
                    ret_send.at[app, slot, q], hand_recv.at[app, slot - 1, q],
                    row_at(1), off,
                ).start()

    def deliver(app, slot):
        shift = off * slots + slot
        for q in range(n_off):
            if slot < slots - 1:
                @pl.when(odd)
                def _():
                    where = hand.at[app, slot, q]
                    copy(where, where, hand_recv.at[app, slot, q],
                         hand_recv.at[app, slot, q], row_at(1), off).wait_recv()
                    back[app, slot, q] = back[app, slot, q] + hand[app, slot, q]

            def away():
                copy(
                    back.at[app, slot, q], ret.at[app, off, slot],
                    ret_send.at[app, slot, q], ret_recv.at[app, off, slot],
                    row_at(shift), q,
                ).start()

            pl.when(odd if slot else shift != 0)(away)

    def forward(apps, slot, first):
        count = k * len(apps)
        for c in range(width // chunk):
            at = pl.ds(c * chunk, chunk)
            both = coarse(split[slot, : 2 * count, :], high[slot, at, :], NT)
            rest = coarse(split[slot, :count, :], low[slot, at, :], NT)
            term = both[:count] + both[count:] + rest
            q, place = (c * chunk) // part, (c * chunk) % part
            where = pl.ds(place, chunk)
            for index, app in enumerate(apps):
                one = term[index * k : (index + 1) * k]
                if first:
                    direct[app, q, :, where] = one
                else:
                    direct[app, q, :, where] = direct[app, q, :, where] + one

    rows = 32
    for slot in order:
        limit = live_ref[0, slot]

        def cut(index, carry):
            start = pl.multiple_of(index * rows, rows)
            ids = lax.broadcasted_iota(jnp.int32, (rows, width), 0) + start
            value = jnp.where(ids < limit, raw[slot, pl.ds(start, rows), :], 0.0)
            hi, lo = halves(value)
            high[slot, pl.ds(start, rows), :] = hi
            low[slot, pl.ds(start, rows), :] = lo
            return carry

        for piece, one in enumerate(loads[slot]):
            one.wait()
            lax.fori_loop(piece * span // rows, (piece + 1) * span // rows, cut, 0)
        transposed((0,), slot)
        deliver(0, slot)

    def collect(dst, own, send, recv, use):
        for slot in range(slots):
            if slot == 0:
                @pl.when(off == 0)
                def _():
                    dst[0] = own[...]

                @pl.when(off != 0)
                def _():
                    gathered(0, dst, recv)
            else:
                gathered(slot, dst, recv)
            if slot == slots - 2:
                relay(dst, send, recv, begin)
            use(slot)

    def eye():
        return (
            lax.broadcasted_iota(jnp.int32, (k, k), 0)
            == lax.broadcasted_iota(jnp.int32, (k, k), 1)
        ).astype(jnp.float32)

    def exchange(app):
        @pl.when(off == 0)
        def _():
            for q in range(n_off):
                direct[app, q] = direct[app, q] + back[app, 0, q]

        for step in range(1, n_off):
            copy(
                direct.at[app, peer(step)], ret.at[app, off, slots],
                ret_send.at[app, slots, step], ret_recv.at[app, off, slots],
                me, peer(step),
            ).start()

    def image(app, value):
        acc[...] = energy_ref[:, cols(off)] * value + direct[app, off]
        for group in range(n_off):
            for slot in range(slots):
                def take():
                    where = ret.at[app, group, slot]
                    copy(where, where, ret_send.at[app, 0, 0], ret_recv.at[app, group, slot],
                         row_at(1), off).wait_recv()
                    acc[...] = acc[...] + ret[app, group, slot]

                if slot:
                    pl.when(lax.rem(me + group * slots + slot, 2) == 1)(take)
                elif group:
                    take()
        total = acc[...]
        for step in range(1, n_off):
            where = ret.at[app, peer(step), slots]
            copy(where, where, ret_send.at[app, 0, 0], ret_recv.at[app, peer(step), slots],
                 row_at(1), off).wait_recv()
            total = total + ret[app, peer(step), slots]
        return total

    def use_first(slot):
        put_split(slot, near[slot, :k, :])
        forward((0,), slot, slot == 0)

    collect(near, mine, fetch_relay, fetch_recv, use_first)
    exchange(0)

    put_split(slots, precond_ref[...] * vec_ref[...])
    for slot in order:
        transposed((1,), slot)
    for slot in range(slots):
        put_split(slot, near[slot, k : k + 1, :] * near[slot, :k, :])
        forward((1,), slot, slot == 0)

    p_part = precond_ref[:, cols(off)]

    for it in range(ITERS):
        last = it == ITERS - 1
        if it == 0:
            x_part = vec_ref[:, cols(off)]
            total = image(0, x_part)
        else:
            x_part = out_ref[:, cols(off)]
            total_a = image(2, part_a[0])
            total = triple(both_fix, jnp.concatenate([total_a, total_b], axis=0))
        a_part = x_part - p_part * total
        part_a[it] = a_part
        own_a[it, :, cols(off)] = a_part
        for step in range(1, n_off):
            copy(
                part_a.at[it], own_a.at[it, :, cols(off)],
                peer_send.at[it, step], peer_recv.at[it, off], me, peer(step),
            ).start()
        if not last:
            spread(part_a.at[it], near_a, share_send, share_recv, begin)
            for slot in order:
                deliver(1, slot)
            exchange(1)

        ab = jnp.concatenate([a_part, p_part * x_part], axis=0)
        inner = triple(ab, ab, NT)
        xy = triple(x_part, total, NT)
        low_half = jnp.concatenate([xy, inner[k:, k:]], axis=1)
        packed = jnp.concatenate([inner[:k, :], low_half], axis=0)
        for t in range(team):
            gram[it, t] = packed[t * grow : (t + 1) * grow, :]

        def mate(step):
            index = lax.rem(spot + step, team)
            return index, base + index // n_off, lax.rem(index, n_off)

        for step in range(1, team):
            index, row, col = mate(step)
            copy(
                gram.at[it, index], gram_in.at[it, spot], gs_send.at[it, step],
                gs_recv.at[it, spot], row, col,
            ).start()
        for step in range(1, n_off):
            where = own_a.at[it, :, cols(peer(step))]
            copy(where, where, peer_send.at[it, step], peer_recv.at[it, peer(step)],
                 row_at(1), off).wait_recv()
        if not last:
            put_split(slots, own_a[0])
            for slot in order:
                transposed((2,), slot)
                deliver(2, slot)
        piece = gram[it, spot]
        for step in range(1, team):
            index = mate(step)[0]
            where = gram_in.at[it, index]
            copy(where, where, gs_send.at[it, step], gs_recv.at[it, index],
                 row_at(1), off).wait_recv()
            piece = piece + gram_in[it, index]
        gram_off[it, floor] = piece
        for step in range(1, floors):
            copy(
                gram_off.at[it, floor], gram_off.at[it, floor], go_send.at[it, step],
                go_recv.at[it, floor], row_at(step * block), off,
            ).start()

        if not last:
            def use_second(slot):
                put_split(slot, near_a[slot])
                forward((2,), slot, slot == 0)

            collect(near_a, own_a.at[0], share_relay, share_recv, use_second)
            exchange(2)
        for step in range(1, floors):
            index = lax.rem(floor + step, floors)
            where = gram_off.at[it, index]
            copy(where, where, go_send.at[it, step], go_recv.at[it, index],
                 row_at(1), off).wait_recv()
        piece = gram_off[it, 0]
        for index in range(1, floors):
            piece = piece + gram_off[it, index]
        gram_sum[it] = piece
        gram_all[it, spot] = piece
        for step in range(1, team):
            index, row, col = mate(step)
            copy(
                gram_sum.at[it], gram_all.at[it, spot], ga_send.at[it, step],
                ga_recv.at[it, spot], row, col,
            ).start()
        if not last:
            total_b = image(1, p_part * x_part)
        for step in range(1, team):
            index = mate(step)[0]
            where = gram_all.at[it, index]
            copy(where, where, ga_send.at[it, step], ga_recv.at[it, index],
                 row_at(1), off).wait_recv()
        full = gram_all[it].reshape(2 * k, 2 * k) / total_rows
        turned = full.T
        ritz, ritz_t = full[k:, :k], turned[:k, k:]
        aa, cross, cross_t, bb = full[:k, :k], full[:k, k:], turned[k:, :k], full[k:, k:]
        mixed = triple(jnp.concatenate([cross, bb], axis=0), ritz)
        overlap = aa + mixed[:k] + triple(ritz_t, cross_t + mixed[k:])
        fix = 1.5 * eye() - 0.5 * overlap
        both_fix = jnp.concatenate([fix, triple(fix, ritz_t)], axis=1)

        state = vec_ref if it == 0 else out_ref
        out_ref[...] = triple(
            both_fix,
            jnp.concatenate([own_a[it], precond_ref[...] * state[...]], axis=0),
        )
        if last:
            ritz_ref[...] = ritz

    spread(mine.at[:, cols(off)], near, fetch_send, fetch_recv, finish)
    relay(near, fetch_relay, fetch_recv, finish)
    spread(part_a.at[0], near_a, share_send, share_recv, finish)
    relay(near_a, share_relay, share_recv, finish)
    for app in range(APPS):
        for slot in range(slots):
            for q in range(n_off):
                def gone():
                    copy(back.at[app, slot, q], ret.at[app, off, slot],
                         ret_send.at[app, slot, q], ret_recv.at[app, off, slot],
                         row_at(1), q).wait_send()

                if slot:
                    gone()
                else:
                    pl.when(off != 0)(gone)
        for step in range(1, n_off):
            copy(direct.at[app, 0], ret.at[app, off, slots], ret_send.at[app, slots, step],
                 ret_recv.at[app, off, slots], me, peer(step)).wait_send()
    for it in range(ITERS):
        for step in range(1, n_off):
            copy(part_a.at[it], part_a.at[it], peer_send.at[it, step],
                 peer_recv.at[it, off], me, peer(step)).wait_send()

        for step in range(1, team):
            copy(gram_sum.at[it], gram_sum.at[it], gs_send.at[it, step],
                 gs_recv.at[it, 0], row_at(1), off).wait_send()
            copy(gram_sum.at[it], gram_sum.at[it], ga_send.at[it, step],
                 ga_recv.at[it, 0], row_at(1), off).wait_send()
        for step in range(1, floors):
            copy(gram_sum.at[it], gram_sum.at[it], go_send.at[it, step],
                 go_recv.at[it, 0], row_at(1), off).wait_send()


def hand_over(basis_in, ritz_in, basis_out, ritz_out, sems):
    moves = [
        pltpu.make_async_copy(basis_in, basis_out, sems.at[0]),
        pltpu.make_async_copy(ritz_in, ritz_out, sems.at[1]),
    ]
    for one in moves:
        one.start()
    for one in moves:
        one.wait()


def local(n, n_off, vectors, tiles, live, energies, precond):
    k, width = vectors.shape
    slots = tiles.shape[1] // width
    part = width // n_off
    _, team, floors, grow = shares(n, n_off, k)
    outside = pl.BlockSpec(memory_space=pltpu.HBM)
    f32, b16 = jnp.float32, jnp.bfloat16
    vmem, dma = pltpu.VMEM, pltpu.SemaphoreType.DMA
    inside = pl.BlockSpec(memory_space=pltpu.VMEM)
    basis, ritz = pl.pallas_call(
        functools.partial(kernel, n, n_off, slots, float(width * n)),
        out_shape=(
            jax.ShapeDtypeStruct((k, width), f32),
            jax.ShapeDtypeStruct((k, k), f32),
        ),
        in_specs=[outside] * 5,
        out_specs=(inside, inside),
        scratch_shapes=[
            vmem((k, width), f32),
            pltpu.SMEM((1, slots), jnp.int32),
            vmem((1, width), f32),
            vmem((1, width), f32),
            vmem((k, part), f32),
            vmem((APPS, slots, n_off, k, part), f32),
            vmem((slots, width, width), f32),
            vmem((slots, width, width), b16),
            vmem((slots, width, width), b16),
            vmem((k + 8, width), f32),
            vmem((slots, k + 8, width), f32),
            vmem((slots + 1, 2 * k, width), b16),
            vmem((APPS, n_off, k, part), f32),
            vmem((APPS, slots, n_off, k, part), f32),
            vmem((APPS, n_off, slots + 1, k, part), f32),
            vmem((ITERS, k, part), f32),
            vmem((ITERS, k, width), f32),
            vmem((slots, k, width), f32),
            vmem((ITERS, team, grow, 2 * k), f32),
            vmem((ITERS, team, grow, 2 * k), f32),
            vmem((ITERS, floors, grow, 2 * k), f32),
            vmem((ITERS, grow, 2 * k), f32),
            vmem((ITERS, team, grow, 2 * k), f32),
            dma((slots + 4,)),
            dma((slots, width // SPAN)),
            dma((APPS, slots, n_off)),
            dma((slots, n_off)),
            dma((slots, n_off)),
            dma((n_off * slots,)),
            dma((slots, n_off)),
            dma((APPS, slots + 1, n_off)),
            dma((APPS, n_off, slots + 1)),
            dma((n_off * slots,)),
            dma((slots, n_off)),
            dma((ITERS, n_off)),
            dma((ITERS, n_off)),
            dma((ITERS, team)),
            dma((ITERS, team)),
            dma((ITERS, floors)),
            dma((ITERS, floors)),
            dma((ITERS, team)),
            dma((ITERS, team)),
        ],
        compiler_params=pltpu.CompilerParams(
            collective_id=0, has_side_effects=True, vmem_limit_bytes=GRANT
        ),
    )(vectors, tiles, live, energies[None, :], precond[None, :])
    return pl.pallas_call(
        hand_over,
        out_shape=(
            jax.ShapeDtypeStruct((k, width), f32),
            jax.ShapeDtypeStruct((k, k), f32),
        ),
        in_specs=[inside] * 2,
        out_specs=(outside, outside),
        scratch_shapes=[dma((2,))],
        compiler_params=pltpu.CompilerParams(vmem_limit_bytes=GRANT),
    )(basis, ritz)


def solution(mesh):
    placed = (P(None, "row"), P("row", "off"), P("row", "off"), P("row"), P("row"))
    return jax.shard_map(
        functools.partial(local, mesh.shape["row"], mesh.shape["off"]),
        mesh=mesh, in_specs=placed, out_specs=(P(None, "row"), P()), check_vma=False,
    )
```

```python
import functools

import jax
import jax.numpy as jnp
from jax import lax
from jax.experimental import pallas as pl
from jax.experimental.pallas import tpu as pltpu
from jax.sharding import PartitionSpec as P

ITERS = 2
APPS = 3
SPAN = 128
GRANT = 60 * 1024 * 1024
MESH = pl.DeviceIdType.MESH
NN = (((1,), (0,)), ((), ()))
NT = (((1,), (1,)), ((), ()))


def coarse(left, right, dims):
    return lax.dot_general(left, right, dims, preferred_element_type=jnp.float32)


def halves(value):
    high = value.astype(jnp.bfloat16)
    low = (value - high.astype(jnp.float32)).astype(jnp.bfloat16)
    return high, low


def triple(left, right, dims=NN):
    left_hi, left_lo = halves(left)
    right_hi, right_lo = halves(right)
    count = left.shape[0]
    both = coarse(jnp.concatenate([left_hi, left_lo], axis=0), right_hi, dims)
    return both[:count] + both[count:] + coarse(left_hi, right_lo, dims)


def shares(n, n_off, k):
    block = 4 if n % 4 == 0 else 1
    while 2 * k % (block * n_off):
        block //= 2
    team = block * n_off
    return block, team, n // block, 2 * k // team


def kernel(
    n, n_off, slots, total_rows,
    vec_hbm, tiles_ref, live_hbm, energy_hbm, precond_hbm,
    out_ref, ritz_ref,
    vec_ref, live_ref, energy_ref, precond_ref, acc, hand,
    raw, high, low, mine, near, split, direct, back, ret, part_a, own_a, near_a,
    gram, gram_in, gram_off, gram_sum, gram_all,
    load_sem, tile_sem, hand_recv, fetch_relay, share_relay, fetch_send, fetch_recv, ret_send, ret_recv, share_send, share_recv,
    peer_send, peer_recv, gs_send, gs_recv, go_send, go_recv, ga_send, ga_recv,
):
    me = lax.axis_index("row")
    off = lax.axis_index("off")
    k, width = vec_ref.shape
    part = width // n_off
    chunk = min(256, part)
    block, team, floors, grow = shares(n, n_off, k)
    floor, base = me // block, me - lax.rem(me, block)
    spot = lax.rem(me, block) * n_off + off
    devices = n * n_off
    flat_me = me * n_off + off
    odd = lax.rem(me, 2) == 1
    small = devices <= 32

    def copy(src, dst, send, recv, row, col):
        return pltpu.make_async_remote_copy(
            src_ref=src, dst_ref=dst, send_sem=send, recv_sem=recv,
            device_id=(row, col), device_id_type=MESH,
        )

    def row_at(shift):
        return lax.rem(me + shift + n, n)

    def peer(step):
        return lax.rem(off + step, n_off)

    def cols(index):
        return pl.ds(pl.multiple_of(index * part, part), part)

    heads = [
        pltpu.make_async_copy(src, dst, load_sem.at[slots + index])
        for index, (src, dst) in enumerate(
            ((vec_hbm, vec_ref), (precond_hbm, precond_ref),
             (energy_hbm, energy_ref), (live_hbm, live_ref))
        )
    ]
    for one in heads:
        one.start()
    order = list(range(slots - 1, -1, -1))
    span = SPAN
    loads = [
        [
            pltpu.make_async_copy(
                tiles_ref.at[pl.ds(piece * span, span), pl.ds(slot * width, width)],
                raw.at[slot, pl.ds(piece * span, span), :], tile_sem.at[slot, piece],
            )
            for piece in range(width // span)
        ]
        for slot in range(slots)
    ]
    for slot in order:
        for one in loads[slot]:
            one.start()

    barrier = pltpu.get_barrier_semaphore()

    def greet(step, carry):
        flat = lax.rem(flat_me + step, devices)
        pl.semaphore_signal(
            barrier, inc=1, device_id=(flat // n_off, lax.rem(flat, n_off)),
            device_id_type=MESH,
        )
        return carry

    lax.fori_loop(1, devices, greet, 0, unroll=small)
    for one in heads:
        one.wait()
    mine[:k, :] = vec_ref[...]
    mine[k:, :] = jnp.broadcast_to(precond_ref[...], (mine.shape[0] - k, width))
    pl.semaphore_wait(barrier, devices - 1)

    def spread(src, dst, send, recv, act):
        for group in range(n_off):
            for slot in range(slots):
                shift = group * slots + slot

                def step():
                    one = copy(
                        src, dst.at[slot, :, cols(off)], send.at[shift],
                        recv.at[slot, off], row_at(-shift), group,
                    )
                    act(one)

                if slot:
                    pl.when(lax.rem(me + shift, 2) == 1)(step)
                elif shift:
                    step()

    def relay(dst, send, recv, act):
        @pl.when(odd)
        def _():
            for slot in range(slots - 1):
                for q in range(n_off):
                    act(copy(
                        dst.at[slot, :, cols(q)], dst.at[slot + 1, :, cols(q)],
                        send.at[slot, q], recv.at[slot + 1, q], row_at(-1), off,
                    ))

    def begin(one):
        one.start()

    def finish(one):
        one.wait_send()

    def gathered(slot, dst, recv):
        for step in range(n_off):
            where = dst.at[slot, :, cols(step)]
            copy(where, where, recv.at[slot, step], recv.at[slot, step],
                 row_at(1), off).wait_recv()

    spread(mine.at[:, cols(off)], near, fetch_send, fetch_recv, begin)

    def put_split(where, value):
        count = value.shape[0]
        hi, lo = halves(value)
        split[where, :count, :] = hi
        split[where, count : 2 * count, :] = lo

    put_split(slots, vec_ref[...])

    def transposed(apps, slot):
        count = k * len(apps)
        for q in range(n_off):
            for c in range(part // chunk):
                at = pl.ds(q * part + c * chunk, chunk)
                both = coarse(split[slots, : 2 * count, :], high[slot, :, at], NN)
                rest = coarse(split[slots, :count, :], low[slot, :, at], NN)
                term = both[:count] + both[count:] + rest
                for index, app in enumerate(apps):
                    back[app, slot, q, :, pl.ds(c * chunk, chunk)] = (
                        term[index * k : (index + 1) * k]
                    )
            for app in apps:
                hand_on(app, slot, q)

    def hand_on(app, slot, q):
        if slot:
            @pl.when(jnp.logical_not(odd))
            def _():
                copy(
                    back.at[app, slot, q], hand.at[app, slot - 1, q],
                    ret_send.at[app, slot, q], hand_recv.at[app, slot - 1, q],
                    row_at(1), off,
                ).start()

    def deliver(app, slot):
        shift = off * slots + slot
        for q in range(n_off):
            if slot < slots - 1:
                @pl.when(odd)
                def _():
                    where = hand.at[app, slot, q]
                    copy(where, where, hand_recv.at[app, slot, q],
                         hand_recv.at[app, slot, q], row_at(1), off).wait_recv()
                    back[app, slot, q] = back[app, slot, q] + hand[app, slot, q]

            def away():
                copy(
                    back.at[app, slot, q], ret.at[app, off, slot],
                    ret_send.at[app, slot, q], ret_recv.at[app, off, slot],
                    row_at(shift), q,
                ).start()

            pl.when(odd if slot else shift != 0)(away)

    def forward(apps, slot, first):
        count = k * len(apps)
        for c in range(width // chunk):
            at = pl.ds(c * chunk, chunk)
            both = coarse(split[slot, : 2 * count, :], high[slot, at, :], NT)
            rest = coarse(split[slot, :count, :], low[slot, at, :], NT)
            term = both[:count] + both[count:] + rest
            q, place = (c * chunk) // part, (c * chunk) % part
            where = pl.ds(place, chunk)
            for index, app in enumerate(apps):
                one = term[index * k : (index + 1) * k]
                if first:
                    direct[app, q, :, where] = one
                else:
                    direct[app, q, :, where] = direct[app, q, :, where] + one

    rows = 32
    for slot in order:
        limit = live_ref[0, slot]

        def cut(index, carry):
            start = pl.multiple_of(index * rows, rows)
            ids = lax.broadcasted_iota(jnp.int32, (rows, width), 0) + start
            value = jnp.where(ids < limit, raw[slot, pl.ds(start, rows), :], 0.0)
            hi, lo = halves(value)
            high[slot, pl.ds(start, rows), :] = hi
            low[slot, pl.ds(start, rows), :] = lo
            return carry

        for piece, one in enumerate(loads[slot]):
            one.wait()
            lax.fori_loop(piece * span // rows, (piece + 1) * span // rows, cut, 0)
        transposed((0,), slot)
        deliver(0, slot)

    def collect(dst, own, send, recv, use):
        for slot in range(slots):
            if slot == 0:
                @pl.when(off == 0)
                def _():
                    dst[0] = own[...]

                @pl.when(off != 0)
                def _():
                    gathered(0, dst, recv)
            else:
                gathered(slot, dst, recv)
            if slot == slots - 2:
                relay(dst, send, recv, begin)
            use(slot)

    def eye():
        return (
            lax.broadcasted_iota(jnp.int32, (k, k), 0)
            == lax.broadcasted_iota(jnp.int32, (k, k), 1)
        ).astype(jnp.float32)

    def exchange(app):
        @pl.when(off == 0)
        def _():
            for q in range(n_off):
                direct[app, q] = direct[app, q] + back[app, 0, q]

        for step in range(1, n_off):
            copy(
                direct.at[app, peer(step)], ret.at[app, off, slots],
                ret_send.at[app, slots, step], ret_recv.at[app, off, slots],
                me, peer(step),
            ).start()

    def image(app, value):
        acc[...] = energy_ref[:, cols(off)] * value + direct[app, off]
        for group in range(n_off):
            for slot in range(slots):
                def take():
                    where = ret.at[app, group, slot]
                    copy(where, where, ret_send.at[app, 0, 0], ret_recv.at[app, group, slot],
                         row_at(1), off).wait_recv()
                    acc[...] = acc[...] + ret[app, group, slot]

                if slot:
                    pl.when(lax.rem(me + group * slots + slot, 2) == 1)(take)
                elif group:
                    take()
        total = acc[...]
        for step in range(1, n_off):
            where = ret.at[app, peer(step), slots]
            copy(where, where, ret_send.at[app, 0, 0], ret_recv.at[app, peer(step), slots],
                 row_at(1), off).wait_recv()
            total = total + ret[app, peer(step), slots]
        return total

    def use_first(slot):
        put_split(slot, near[slot, :k, :])
        forward((0,), slot, slot == 0)

    collect(near, mine, fetch_relay, fetch_recv, use_first)
    exchange(0)

    put_split(slots, precond_ref[...] * vec_ref[...])
    for slot in order:
        transposed((1,), slot)
        deliver(1, slot)
    for slot in range(slots):
        put_split(slot, near[slot, k : k + 1, :] * near[slot, :k, :])
        forward((1,), slot, slot == 0)
    exchange(1)

    p_part = precond_ref[:, cols(off)]

    for it in range(ITERS):
        last = it == ITERS - 1
        if it == 0:
            x_part = vec_ref[:, cols(off)]
            total = image(0, x_part)
        else:
            x_part = out_ref[:, cols(off)]
            total_a = image(2, part_a[0])
            total = triple(both_fix, jnp.concatenate([total_a, total_b], axis=0))
        a_part = x_part - p_part * total
        part_a[it] = a_part
        own_a[it, :, cols(off)] = a_part
        for step in range(1, n_off):
            copy(
                part_a.at[it], own_a.at[it, :, cols(off)],
                peer_send.at[it, step], peer_recv.at[it, off], me, peer(step),
            ).start()
        if not last:
            spread(part_a.at[it], near_a, share_send, share_recv, begin)

        ab = jnp.concatenate([a_part, p_part * x_part], axis=0)
        inner = triple(ab, ab, NT)
        xy = triple(x_part, total, NT)
        low_half = jnp.concatenate([xy, inner[k:, k:]], axis=1)
        packed = jnp.concatenate([inner[:k, :], low_half], axis=0)
        for t in range(team):
            gram[it, t] = packed[t * grow : (t + 1) * grow, :]

        def mate(step):
            index = lax.rem(spot + step, team)
            return index, base + index // n_off, lax.rem(index, n_off)

        for step in range(1, team):
            index, row, col = mate(step)
            copy(
                gram.at[it, index], gram_in.at[it, spot], gs_send.at[it, step],
                gs_recv.at[it, spot], row, col,
            ).start()
        for step in range(1, n_off):
            where = own_a.at[it, :, cols(peer(step))]
            copy(where, where, peer_send.at[it, step], peer_recv.at[it, peer(step)],
                 row_at(1), off).wait_recv()
        if not last:
            put_split(slots, own_a[0])
            for slot in order:
                transposed((2,), slot)
                deliver(2, slot)
        piece = gram[it, spot]
        for step in range(1, team):
            index = mate(step)[0]
            where = gram_in.at[it, index]
            copy(where, where, gs_send.at[it, step], gs_recv.at[it, index],
                 row_at(1), off).wait_recv()
            piece = piece + gram_in[it, index]
        gram_off[it, floor] = piece
        for step in range(1, floors):
            copy(
                gram_off.at[it, floor], gram_off.at[it, floor], go_send.at[it, step],
                go_recv.at[it, floor], row_at(step * block), off,
            ).start()

        if not last:
            def use_second(slot):
                put_split(slot, near_a[slot])
                forward((2,), slot, slot == 0)

            collect(near_a, own_a.at[0], share_relay, share_recv, use_second)
            exchange(2)
        for step in range(1, floors):
            index = lax.rem(floor + step, floors)
            where = gram_off.at[it, index]
            copy(where, where, go_send.at[it, step], go_recv.at[it, index],
                 row_at(1), off).wait_recv()
        piece = gram_off[it, 0]
        for index in range(1, floors):
            piece = piece + gram_off[it, index]
        gram_sum[it] = piece
        gram_all[it, spot] = piece
        for step in range(1, team):
            index, row, col = mate(step)
            copy(
                gram_sum.at[it], gram_all.at[it, spot], ga_send.at[it, step],
                ga_recv.at[it, spot], row, col,
            ).start()
        if not last:
            total_b = image(1, p_part * x_part)
        for step in range(1, team):
            index = mate(step)[0]
            where = gram_all.at[it, index]
            copy(where, where, ga_send.at[it, step], ga_recv.at[it, index],
                 row_at(1), off).wait_recv()
        full = gram_all[it].reshape(2 * k, 2 * k) / total_rows
        turned = full.T
        ritz, ritz_t = full[k:, :k], turned[:k, k:]
        aa, cross, cross_t, bb = full[:k, :k], full[:k, k:], turned[k:, :k], full[k:, k:]
        mixed = triple(jnp.concatenate([cross, bb], axis=0), ritz)
        overlap = aa + mixed[:k] + triple(ritz_t, cross_t + mixed[k:])
        fix = 1.5 * eye() - 0.5 * overlap
        both_fix = jnp.concatenate([fix, triple(fix, ritz_t)], axis=1)

        state = vec_ref if it == 0 else out_ref
        out_ref[...] = triple(
            both_fix,
            jnp.concatenate([own_a[it], precond_ref[...] * state[...]], axis=0),
        )
        if last:
            ritz_ref[...] = ritz

    spread(mine.at[:, cols(off)], near, fetch_send, fetch_recv, finish)
    relay(near, fetch_relay, fetch_recv, finish)
    spread(part_a.at[0], near_a, share_send, share_recv, finish)
    relay(near_a, share_relay, share_recv, finish)
    for app in range(APPS):
        for slot in range(slots):
            for q in range(n_off):
                def gone():
                    copy(back.at[app, slot, q], ret.at[app, off, slot],
                         ret_send.at[app, slot, q], ret_recv.at[app, off, slot],
                         row_at(1), q).wait_send()

                if slot:
                    gone()
                else:
                    pl.when(off != 0)(gone)
        for step in range(1, n_off):
            copy(direct.at[app, 0], ret.at[app, off, slots], ret_send.at[app, slots, step],
                 ret_recv.at[app, off, slots], me, peer(step)).wait_send()
    for it in range(ITERS):
        for step in range(1, n_off):
            copy(part_a.at[it], part_a.at[it], peer_send.at[it, step],
                 peer_recv.at[it, off], me, peer(step)).wait_send()

        for step in range(1, team):
            copy(gram_sum.at[it], gram_sum.at[it], gs_send.at[it, step],
                 gs_recv.at[it, 0], row_at(1), off).wait_send()
            copy(gram_sum.at[it], gram_sum.at[it], ga_send.at[it, step],
                 ga_recv.at[it, 0], row_at(1), off).wait_send()
        for step in range(1, floors):
            copy(gram_sum.at[it], gram_sum.at[it], go_send.at[it, step],
                 go_recv.at[it, 0], row_at(1), off).wait_send()


def hand_over(basis_in, ritz_in, basis_out, ritz_out, sems):
    moves = [
        pltpu.make_async_copy(basis_in, basis_out, sems.at[0]),
        pltpu.make_async_copy(ritz_in, ritz_out, sems.at[1]),
    ]
    for one in moves:
        one.start()
    for one in moves:
        one.wait()


def local(n, n_off, vectors, tiles, live, energies, precond):
    k, width = vectors.shape
    slots = tiles.shape[1] // width
    part = width // n_off
    _, team, floors, grow = shares(n, n_off, k)
    outside = pl.BlockSpec(memory_space=pltpu.HBM)
    f32, b16 = jnp.float32, jnp.bfloat16
    vmem, dma = pltpu.VMEM, pltpu.SemaphoreType.DMA
    inside = pl.BlockSpec(memory_space=pltpu.VMEM)
    basis, ritz = pl.pallas_call(
        functools.partial(kernel, n, n_off, slots, float(width * n)),
        out_shape=(
            jax.ShapeDtypeStruct((k, width), f32),
            jax.ShapeDtypeStruct((k, k), f32),
        ),
        in_specs=[outside] * 5,
        out_specs=(inside, inside),
        scratch_shapes=[
            vmem((k, width), f32),
            pltpu.SMEM((1, slots), jnp.int32),
            vmem((1, width), f32),
            vmem((1, width), f32),
            vmem((k, part), f32),
            vmem((APPS, slots, n_off, k, part), f32),
            vmem((slots, width, width), f32),
            vmem((slots, width, width), b16),
            vmem((slots, width, width), b16),
            vmem((k + 8, width), f32),
            vmem((slots, k + 8, width), f32),
            vmem((slots + 1, 2 * k, width), b16),
            vmem((APPS, n_off, k, part), f32),
            vmem((APPS, slots, n_off, k, part), f32),
            vmem((APPS, n_off, slots + 1, k, part), f32),
            vmem((ITERS, k, part), f32),
            vmem((ITERS, k, width), f32),
            vmem((slots, k, width), f32),
            vmem((ITERS, team, grow, 2 * k), f32),
            vmem((ITERS, team, grow, 2 * k), f32),
            vmem((ITERS, floors, grow, 2 * k), f32),
            vmem((ITERS, grow, 2 * k), f32),
            vmem((ITERS, team, grow, 2 * k), f32),
            dma((slots + 4,)),
            dma((slots, width // SPAN)),
            dma((APPS, slots, n_off)),
            dma((slots, n_off)),
            dma((slots, n_off)),
            dma((n_off * slots,)),
            dma((slots, n_off)),
            dma((APPS, slots + 1, n_off)),
            dma((APPS, n_off, slots + 1)),
            dma((n_off * slots,)),
            dma((slots, n_off)),
            dma((ITERS, n_off)),
            dma((ITERS, n_off)),
            dma((ITERS, team)),
            dma((ITERS, team)),
            dma((ITERS, floors)),
            dma((ITERS, floors)),
            dma((ITERS, team)),
            dma((ITERS, team)),
        ],
        compiler_params=pltpu.CompilerParams(
            collective_id=0, has_side_effects=True, vmem_limit_bytes=GRANT
        ),
    )(vectors, tiles, live, energies[None, :], precond[None, :])
    return pl.pallas_call(
        hand_over,
        out_shape=(
            jax.ShapeDtypeStruct((k, width), f32),
            jax.ShapeDtypeStruct((k, k), f32),
        ),
        in_specs=[inside] * 2,
        out_specs=(outside, outside),
        scratch_shapes=[dma((2,))],
        compiler_params=pltpu.CompilerParams(vmem_limit_bytes=GRANT),
    )(basis, ritz)


def solution(mesh):
    placed = (P(None, "row"), P("row", "off"), P("row", "off"), P("row"), P("row"))
    return jax.shard_map(
        functools.partial(local, mesh.shape["row"], mesh.shape["off"]),
        mesh=mesh, in_specs=placed, out_specs=(P(None, "row"), P()), check_vma=False,
    )
```
